128 devices in a mesh: prow: 16 (over x, y), pcol: 8 (over z, core).
Axes of the slice: x: 4, y: 4, z: 4, core: 2. Of those that a mesh axis runs over, the one named last changes fastest.
Arguments:
- matrix: float32 [8, 16, 128, 16, 8, 128], P(None, 'prow', None, None, 'pcol'), may hold values from -6 to 6
- pivots: int32 [2, 128], replicated, may hold values from 0 to 16383, as said below
- block_inverses: float32 [2, 128, 128], replicated, may hold values from -0.046875 to 0.046875
Outputs:
- factored: float32 [8, 16, 128, 16, 8, 128], P(None, 'prow', None, None, 'pcol')
The draws below stay inside these ranges and needn't reach their ends.
Inputs may be any that keep to these rules, and one draw needn't show every extreme that they name: `pivots`: entry j of step k lies in j to 16384 - k * 128 - 1.
All inputs are finite; a program needn't handle non-finite values.
Results may differ from the reference program's by a relative error of at most 0.0001.
Values sent between devices are 32-bit elements; how exact they have to be, the bound alone decides.
A program may use at most 64 MiB of HBM per device.

```python
import jax
import jax.numpy as jnp
from jax import lax

ORDER = 16384
PANEL = 128
STEPS = 2
ROWBLK = 8
COLBLK = 16
N_PROW = 16
N_PCOL = 8


def draw_pivots(key, part):
    key = jax.random.fold_in(key, 7)
    column = jnp.arange(PANEL, dtype=jnp.int32)[None, :]
    step_ids = jnp.arange(STEPS, dtype=jnp.int32)[:, None]
    ceiling = ORDER - step_ids * PANEL
    drawn = jax.random.randint(key, (STEPS, PANEL), column, ceiling, dtype=jnp.int32)
    drawn = drawn.at[0, PANEL - 1].set(ORDER - 1)
    return drawn.at[STEPS - 1, 0].set(0)


def block_scale(rng, shape, shards, least, high):
    def one(position, shards_of):
        steps = jax.random.uniform(jax.random.fold_in(jax.random.fold_in(rng, 6), position), (shards_of,), jnp.float32, least / len(shards), high / len(shards))
        return jnp.repeat(jnp.exp(steps), shape[position] // shards_of).reshape((-1,) + (1,) * (len(shape) - position - 1))

    level = one(*shards[0])
    for cut in shards[1:]:
        level = level * one(*cut)
    return level


def gaussian(rng, extent, deviation, limit, shards=(), kind=jnp.bfloat16):
    result = deviation * jax.random.normal(rng, extent, jnp.float32)
    if shards:
        result = result * block_scale(rng, extent, shards, -0.22, 0.18)
    return jnp.clip(result, -limit, limit).astype(kind)


def setup_inputs(seed: int = 0) -> dict:
    key_of = jax.random.split(jax.random.key(seed), 4)
    return {
        "matrix": gaussian(key_of[0], (ROWBLK, N_PROW, PANEL, COLBLK, N_PCOL, PANEL), 1.0, 6.0, ((1, 16), (4, 8)), jnp.float32),
        "pivots": draw_pivots(jax.random.fold_in(key_of[3], 71), 0),
        "block_inverses": gaussian(key_of[2], (STEPS, PANEL, PANEL), (PANEL * PANEL) ** -0.5, 0.046875, (), jnp.float32),
    }


def swap_order(pivot_row, first_row, total_rows, nblock):
    row_order = jnp.arange(total_rows, dtype=jnp.int32)

    def swap_one(column, row_order):
        slot_top = first_row + column
        slot_low = first_row + pivot_row[column]
        first_src = row_order[slot_top]
        second_src = row_order[slot_low]
        return row_order.at[slot_top].set(second_src).at[slot_low].set(first_src)

    return lax.fori_loop(0, nblock, swap_one, row_order)


def reference(matrix, pivots, block_inverses):
    working = matrix.reshape(ORDER, ORDER)
    for step_index in range(STEPS):
        first_row = step_index * PANEL
        split_at = first_row + PANEL
        row_order = swap_order(pivots[step_index], first_row, ORDER, PANEL)
        moved = jnp.concatenate([first_row + jnp.arange(PANEL, dtype=jnp.int32), (first_row + pivots[step_index]).astype(jnp.int32)])
        working = working.at[moved].set(working[row_order[moved]])
        factor = jnp.dot(working[split_at:, first_row:split_at], block_inverses[step_index], precision=lax.Precision.HIGHEST, preferred_element_type=jnp.float32)
        working = working.at[split_at:, first_row:split_at].set(factor)
        upper_rows = working[first_row:split_at, split_at:]
        update = jnp.dot(factor, upper_rows, precision=lax.Precision.HIGHEST, preferred_element_type=jnp.float32)
        working = working.at[split_at:, split_at:].set(working[split_at:, split_at:] - update)
    return working.reshape(matrix.shape)
```

```python
import functools

import jax
import jax.numpy as jnp
from jax import lax
from jax.experimental import pallas as pl
from jax.experimental.pallas import tpu as pltpu
from jax.sharding import PartitionSpec as P

MESH = pl.DeviceIdType.MESH
NB = 128
NT = 256
DEV = 16
ROWS = 1024
FEW = 2
MANY = 16
MIB = 1 << 20

T_PLACE, T_DST, T_SRC, T_COUNT, T_PICK_FEW, T_PICK_MANY, T_SEND_MANY, T_MOST = range(8)


def iota(shape, dim):
    return lax.broadcasted_iota(jnp.int32, shape, dim)


def fiota(shape, dim):
    return iota(shape, dim).astype(jnp.float32)


def plan_kernel(piv_ref, a_ref, table_ref, send_ref, row_buf, row_smem, sem, row_sem):
    me = lax.axis_index("prow")
    sq = (NT, NT)
    sub, lane = fiota(sq, 0), fiota(sq, 1)
    diag = sub == lane
    lane1 = fiota((1, NT), 1)

    def to_col(row):
        return jnp.sum(jnp.where(diag, row, 0.0), axis=1, keepdims=True)

    piv = piv_ref[...].astype(jnp.float32)
    t_row = jnp.concatenate([piv[0:1, :], piv[1:2, :] + float(NB)], axis=1)
    t_col = to_col(t_row)
    before = sub < lane
    same = t_col == t_row
    last_same = jnp.max(jnp.where(same & before, sub, -1.0), axis=0, keepdims=True)
    later = jnp.max(jnp.where(same & (sub > lane), 1.0, 0.0), axis=0, keepdims=True)
    parent = jnp.max(jnp.where((t_col == lane) & before, sub, -1.0), axis=0, keepdims=True)
    c_row = jnp.where(parent < 0.0, lane1, parent)

    def jump(_, c_row):
        c_col = to_col(c_row)
        return jnp.sum(jnp.where(sub == c_row, c_col, 0.0), axis=0, keepdims=True)

    c_row = lax.fori_loop(0, 8, jump, c_row)
    c_col = to_col(c_row)
    from_swap = jnp.sum(jnp.where(sub == last_same, c_col, 0.0), axis=0, keepdims=True)
    src = jnp.where(last_same < 0.0, t_row, from_swap).astype(jnp.int32)
    owner = (src >> 7) & (DEV - 1)
    local = ((src >> 11) << 7) + (src & (NB - 1))
    owner_row = owner.astype(jnp.float32)
    owner_col = to_col(owner_row)
    less = owner_col < owner_row
    first = jnp.sum(jnp.where(less, 1.0, 0.0), axis=0, keepdims=True).astype(jnp.int32)
    ahead = less | ((owner_col == owner_row) & before)
    pos = jnp.sum(jnp.where(ahead, 1.0, 0.0), axis=0, keepdims=True).astype(jnp.int32)
    rank = pos - first
    most = jnp.max(rank.astype(jnp.float32), axis=1, keepdims=True) + 1.0
    bin_ = pos & (DEV - 1)
    place = bin_ * 16 + (pos >> 4)
    table_ref[T_PLACE : T_PLACE + 1, :] = place
    table_ref[T_MOST : T_MOST + 1, :] = jnp.broadcast_to(most, (1, NT)).astype(jnp.int32)

    mine = owner == me
    local_col = to_col(local.astype(jnp.float32))
    which = rank >> 4
    few = to_col(jnp.where(mine, bin_ * FEW + which, -1).astype(jnp.float32))
    send_few = jnp.sum(jnp.where(few == lane, local_col, 0.0), axis=0, keepdims=True)
    row_buf[0:1, :] = send_few.astype(jnp.int32)
    to_smem = pltpu.make_async_copy(row_buf, row_smem, sem)
    to_smem.start()

    many = to_col(jnp.where(mine, bin_ * MANY + which, -1).astype(jnp.float32))
    send_many = jnp.sum(jnp.where(many == lane, local_col, 0.0), axis=0, keepdims=True)
    table_ref[T_SEND_MANY : T_SEND_MANY + 1, :] = send_many.astype(jnp.int32)

    my_slot = to_col(jnp.where(bin_ == me, pos >> 4, -1).astype(jnp.float32)) == lane
    for row, k in ((T_PICK_FEW, FEW), (T_PICK_MANY, MANY)):
        from_col = to_col((owner * k + which).astype(jnp.float32))
        pick = jnp.sum(jnp.where(my_slot, from_col, 0.0), axis=0, keepdims=True)
        table_ref[row : row + 1, :] = pick.astype(jnp.int32)

    target = t_row.astype(jnp.int32)
    kept = (later < 0.5) & (target >= NT) & (((target >> 7) & (DEV - 1)) == me)
    dst = ((target >> 11) << 7) + (target & (NB - 1))
    c = c_row.astype(jnp.int32)
    within = c & (NB - 1)
    old = NT + (within >> 3) * 16 + (c >> 7) * 8 + (within & 7)
    kept_col = to_col(jnp.where(kept, 1.0, 0.0))
    order = jnp.sum(jnp.where(before & (kept_col > 0.5), 1.0, 0.0), axis=0, keepdims=True)
    slot = to_col(jnp.where(kept, order, -1.0)) == lane
    for row, value in ((T_DST, dst), (T_SRC, old)):
        col = to_col(value.astype(jnp.float32))
        out = jnp.sum(jnp.where(slot, col, 0.0), axis=0, keepdims=True)
        table_ref[row : row + 1, :] = out.astype(jnp.int32)
    count = jnp.sum(jnp.where(kept, 1.0, 0.0), axis=1, keepdims=True)
    table_ref[T_COUNT : T_COUNT + 1, :] = jnp.broadcast_to(count, (1, NT)).astype(jnp.int32)

    to_smem.wait()
    copies = [
        pltpu.make_async_copy(a_ref.at[row_smem[0, i]], send_ref.at[i], row_sem.at[i])
        for i in range(DEV * FEW)
    ]
    for copy in copies:
        copy.start()
    for copy in copies:
        copy.wait()


def plan(pivots, work):
    return pl.pallas_call(
        plan_kernel,
        out_shape=(
            jax.ShapeDtypeStruct((8, NT), jnp.int32),
            jax.ShapeDtypeStruct((DEV * FEW, DEV, NB), jnp.float32),
        ),
        in_specs=[pl.BlockSpec(memory_space=pltpu.VMEM), pl.BlockSpec(memory_space=pl.ANY)],
        out_specs=(pl.BlockSpec(memory_space=pltpu.VMEM), pl.BlockSpec(memory_space=pl.ANY)),
        scratch_shapes=[
            pltpu.VMEM((8, NT), jnp.int32),
            pltpu.SMEM((8, NT), jnp.int32),
            pltpu.SemaphoreType.DMA,
            pltpu.SemaphoreType.DMA((DEV * FEW,)),
        ],
        name="plan",
    )(pivots, work)


def move_kernel(
    k, table_ref, send_ref, a_ref,
    new_out, old_out, panel_out, top_out,
    got, new, old, panel, top,
    s_got, r_got, s_scat, r_scat, s_ag, r_ag, s_z, r_z, s_sib, r_sib, s_loc,
):
    me = lax.axis_index("prow")
    col = lax.axis_index("pcol")
    x, y = me // 4, me % 4
    z, core = col // 2, col % 2
    sends = []

    def at(px, py):
        return (lax.rem(px + 4, 4) * 4 + lax.rem(py + 4, 4), col)

    def remote(src, dst, send_sem, recv_sem, device):
        return pltpu.make_async_remote_copy(
            src_ref=src, dst_ref=dst, send_sem=send_sem, recv_sem=recv_sem,
            device_id=device, device_id_type=MESH,
        )

    offsets = [(dx, dy) for dx in range(4) for dy in range(4) if (dx, dy) != (0, 0)]
    sibling = (me, z * 2 + 1 - core)
    up = (me, lax.rem(z + 1, 4) * 2 + core)
    down = (me, lax.rem(z + 3, 4) * 2 + core)

    mine = pltpu.make_async_copy(a_ref.at[:, 0, :], panel.at[core], s_loc.at[0])
    on_root = z == 0

    @pl.when(on_root)
    def _():
        mine.start()

    barrier = pltpu.get_barrier_semaphore()
    for dx, dy in offsets:
        pl.semaphore_signal(barrier, inc=1, device_id=at(x + dx, y + dy), device_id_type=MESH)
    for device in (sibling, up, down):
        pl.semaphore_signal(barrier, inc=1, device_id=device, device_id_type=MESH)
    pl.semaphore_wait(barrier, len(offsets) + 3)

    for j, (dx, dy) in enumerate(offsets):
        device = at(x + dx, y + dy)
        copy = remote(
            send_ref.at[pl.ds(device[0] * k, k)], got.at[pl.ds(me * k, k)],
            s_got.at[j], r_got.at[j], device,
        )
        copy.start()
        sends.append(copy)
    own = pltpu.make_async_copy(
        send_ref.at[pl.ds(me * k, k)], got.at[pl.ds(me * k, k)], s_loc.at[1]
    )
    own.start()

    def scatter(half):
        copies = []
        for j, (dx, dy) in enumerate(offsets):
            device = at(x + dx, y + dy)
            copies.append(
                remote(
                    a_ref.at[pl.ds(device[0] * 8, 8)],
                    old.at[pl.ds(device[0] * 16 + half * 8, 8)],
                    s_scat.at[j], r_scat.at[half], device,
                )
            )
        return copies

    def scatter_own(half):
        return pltpu.make_async_copy(
            a_ref.at[pl.ds(me * 8, 8)], old.at[pl.ds(me * 16 + half * 8, 8)], s_loc.at[2]
        )

    for half in range(2):

        @pl.when(me == half)
        def _():
            for copy in scatter(half):
                copy.start()
            scatter_own(half).start()

    stage = jnp.where(core == 0, z, lax.rem(4 - z, 4))
    onward = (me, jnp.where(core == 0, lax.rem(z + 1, 4), lax.rem(z + 3, 4)) * 2 + core)
    parts = 4
    size = ROWS // parts

    panel_pieces = []
    for i in range(parts):
        ref = panel.at[core, pl.ds(i * size, size)]
        other = panel.at[1 - core, pl.ds(i * size, size)]
        panel_pieces.append((ref, other, i))
    top_pieces = []
    for i in range(2):
        top_pieces.append((top.at[i, core], top.at[i, 1 - core], parts + i))

    def z_onward(piece):
        ref, _, n = piece
        return remote(ref, ref, s_z.at[n], r_z.at[n], onward)

    def z_sibling(piece):
        ref, _, n = piece
        return remote(ref, ref, s_sib.at[n], r_sib.at[n], sibling)

    def z_step(piece):
        @pl.when(z > 0)
        def _():
            z_onward(piece).wait_recv()

        @pl.when(stage < 3)
        def _():
            z_onward(piece).start()

        z_sibling(piece).start()

    def z_finish(piece):
        ref, other, n = piece

        @pl.when(stage < 3)
        def _():
            z_onward(piece).wait_send()

        z_sibling(piece).wait_send()
        remote(other, other, s_sib.at[n], r_sib.at[n], sibling).wait_recv()

    @pl.when(on_root)
    def _():
        mine.wait()
        for piece in panel_pieces:
            z_onward(piece).start()
            z_sibling(piece).start()

    def ring(axis, step):
        if axis == 0:
            return lax.rem(x + step + 4, 4) * 4 + y
        return x * 4 + lax.rem(y + step + 4, 4)

    def shifted(index, axis, step):
        px, py = index // 4, index % 4
        if axis == 0:
            return lax.rem(px + step + 4, 4) * 4 + py
        return px * 4 + lax.rem(py + step + 4, 4)

    def piece(buf, index, half, part=None):
        if part is None:
            return buf.at[pl.ds(index * 16, 16), pl.ds(half * 8, 8)]
        return buf.at[pl.ds(index * 16 + part * 8, 8), pl.ds(half * 8, 8)]

    class Gather:
        def __init__(self, buf, half, base):
            self.buf, self.half, self.base = buf, half, base
            self.axes = (0, 1) if half == 0 else (1, 0)

        def sem(self, phase, item, role):
            return self.base + phase * (1 + item) * 4 + role

        def start_own(self, phase, item, index):
            axis = self.axes[phase]
            for role, step in ((0, 1), (1, 3)):
                n = self.sem(phase, item, role)
                ref = piece(self.buf, index, self.half)
                copy = remote(ref, ref, s_ag.at[n], r_ag.at[n], (ring(axis, step), col))
                copy.start()
                sends.append(copy)

        def wait_near(self, phase, item, index, role):
            axis = self.axes[phase]
            n = self.sem(phase, item, role)
            came = shifted(index, axis, 3 if role == 0 else 1)
            ref = piece(self.buf, came, self.half)
            remote(ref, ref, s_ag.at[n], r_ag.at[n], (ring(axis, 1), col)).wait_recv()
            n = self.sem(phase, item, 2 + role)
            ref = piece(self.buf, came, self.half, role)
            copy = remote(
                ref, ref, s_ag.at[n], r_ag.at[n], (ring(axis, 1 if role == 0 else 3), col)
            )
            copy.start()
            sends.append(copy)
            return came

        def wait_far(self, phase, item, index):
            axis = self.axes[phase]
            came = shifted(index, axis, 2)
            for role in range(2):
                n = self.sem(phase, item, 2 + role)
                ref = piece(self.buf, came, self.half, role)
                remote(ref, ref, s_ag.at[n], r_ag.at[n], (ring(axis, 1), col)).wait_recv()
            return came

    per = 5 * 4

    def gather(buf, base):
        halves = [Gather(buf, h, base + h * per) for h in range(2)]
        for g in halves:
            g.start_own(0, 0, me)
            g.start_own(1, 0, me)
        items = [[me], [me]]
        for role in range(2):
            for h, g in enumerate(halves):
                came = g.wait_near(0, 0, me, role)
                g.start_own(1, 1 + role, came)
                items[h].append(came)
        for h, g in enumerate(halves):
            came = g.wait_far(0, 0, me)
            g.start_own(1, 3, came)
            items[h].append(came)
        for i in range(4):
            for h, g in enumerate(halves):
                for role in range(2):
                    g.wait_near(1, i, items[h][i], role)
        for i in range(4):
            for h, g in enumerate(halves):
                g.wait_far(1, i, items[h][i])

    for j, (dx, dy) in enumerate(offsets):
        sender = at(x - dx, y - dy)[0]
        remote(
            send_ref.at[pl.ds(0, k)], got.at[pl.ds(sender * k, k)],
            s_got.at[j], r_got.at[j], at(x + dx, y + dy),
        ).wait_recv()
    own.wait()
    pick_row = T_PICK_FEW if k == FEW else T_PICK_MANY
    for s in range(16):
        new[me * 16 + s] = got[table_ref[pick_row, s]]

    for half in range(2):
        part = old.at[pl.ds(me * 16 + half * 8, 8)]

        @pl.when(me == half)
        def _():
            scatter_own(half).wait()
            for copy in scatter(half):
                copy.wait_send()

        @pl.when(me != half)
        def _():
            remote(
                a_ref.at[pl.ds(0, 8)], part, s_scat.at[0], r_scat.at[half], at(x + 1, y)
            ).wait_recv()

    gather(new, 0)

    @pl.when(z > 0)
    def _():
        for p in panel_pieces:
            z_step(p)

    gather(old, 2 * per)

    @pl.when(on_root)
    def _():
        for i, buf in enumerate((new, old)):
            top[i, core] = buf.reshape(NT * DEV, NB)[pl.ds(0, NT, stride=DEV), :]

    for p in top_pieces:
        z_step(p)
    for p in panel_pieces + top_pieces:
        z_finish(p)
    outs = [
        pltpu.make_async_copy(a, b, s_loc.at[3 + i])
        for i, (a, b) in enumerate(
            ((new, new_out), (old, old_out), (panel, panel_out), (top, top_out))
        )
    ]
    for copy in outs:
        copy.start()
    for copy in sends:
        copy.wait_send()
    for copy in outs:
        copy.wait()


def move(k, table, send, work):
    shapes = (
        (NT, DEV, NB),
        (NT, DEV, NB),
        (2, ROWS, NB),
        (2, 2, NT, NB),
    )
    dma = pltpu.SemaphoreType.DMA
    ag = 4 * 20
    return pl.pallas_call(
        functools.partial(move_kernel, k),
        out_shape=tuple(jax.ShapeDtypeStruct(s, jnp.float32) for s in shapes),
        in_specs=[
            pl.BlockSpec(memory_space=pltpu.SMEM),
            pl.BlockSpec(memory_space=pl.ANY),
            pl.BlockSpec(memory_space=pl.ANY),
        ],
        out_specs=tuple(pl.BlockSpec(memory_space=pl.ANY) for _ in shapes),
        scratch_shapes=[pltpu.VMEM((DEV * k, DEV, NB), jnp.float32)]
        + [pltpu.VMEM(s, jnp.float32) for s in shapes]
        + [
            dma((15,)), dma((15,)), dma((15,)), dma((2,)), dma((ag,)), dma((ag,)),
            dma((6,)), dma((6,)), dma((6,)), dma((6,)), dma((7,)),
        ],
        compiler_params=pltpu.CompilerParams(
            collective_id=k, has_side_effects=True, vmem_limit_bytes=24 * MIB
        ),
        name=f"move_{k}",
    )(table, send, work)


def split(a):
    hi = a.astype(jnp.bfloat16)
    return hi, (a - hi.astype(jnp.float32)).astype(jnp.bfloat16)


def dot(a, b):
    return jnp.dot(a, b, preferred_element_type=jnp.float32)


def dot3(a, b):
    return dot(a[0], b[0]) + (dot(a[0], b[1]) + dot(a[1], b[0]))


CHUNKS = 4
CROWS = ROWS // CHUNKS


def update_kernel(
    table_ref, inv_ref, place_ref, a_ref, new_ref, old_ref, panel_ref, top_ref,
    out_ref,
    a, rows, panel, top, b_hi, b_lo, g_hi, g_lo, sems,
):
    me = lax.axis_index("prow")
    col = lax.axis_index("pcol")
    loads = [
        pltpu.make_async_copy(panel_ref, panel, sems.at[0]),
        pltpu.make_async_copy(top_ref, top, sems.at[1]),
        pltpu.make_async_copy(new_ref, rows.at[pl.ds(0, NT)], sems.at[2]),
        pltpu.make_async_copy(old_ref, rows.at[pl.ds(NT, NT)], sems.at[3]),
    ]
    a_loads = [
        pltpu.make_async_copy(
            a_ref.at[pl.ds(i * CROWS, CROWS)], a.at[pl.ds(i * CROWS, CROWS)], sems.at[4 + i]
        )
        for i in range(CHUNKS)
    ]
    for copy in loads + a_loads:
        copy.start()
    loads[0].wait()
    loads[1].wait()

    count = table_ref[T_COUNT, 0]

    def fix_panel(dst, src):
        kind, row = src // NT, lax.rem(src, NT)
        for p in range(2):
            panel[p, pl.ds(dst, 1), :] = top[kind, p, pl.ds(row, 1), :]

    def fix_row(dst, src):
        a[dst] = rows[src]

    def fix_all(fix):
        @pl.when(me < 2)
        def _():
            @pl.loop(0, NB)
            def _(i):
                fix(i, table_ref[T_PLACE, me * NB + i])

        @pl.loop(0, count)
        def _(i):
            fix(table_ref[T_DST, i], table_ref[T_SRC, i])

    fix_all(fix_panel)

    place = place_ref[T_PLACE : T_PLACE + 1, :]
    order_t = jnp.where(iota((NT, NT), 0) == place, 1.0, 0.0).astype(jnp.bfloat16)

    def pick(lo, val):
        return lax.dot_general(
            order_t[:, lo : lo + NB], val, (((0,), (0,)), ((), ())),
            preferred_element_type=jnp.float32,
        )

    inv = [split(inv_ref[s]) for s in range(2)]
    u_split = split(top[0, 1])
    u0p = tuple(pick(0, v).astype(jnp.bfloat16) for v in u_split)
    p_split = split(top[0, 0])
    l0b = dot3(tuple(pick(NB, v).astype(jnp.bfloat16) for v in p_split), inv[0])
    l0b = split(l0b)

    for i in range(CHUNKS):
        part = pl.ds(i * CROWS, CROWS)
        l0 = dot3(split(panel[0, part, :]), inv[0])
        if i == 0:
            top_rows = iota((CROWS, NB), 0) < NB
            l0 = jnp.where(top_rows & (me == 0), 0.0, l0)
        rest = panel[1, part, :] - dot3(split(l0), u0p)
        l1 = dot3(split(rest), inv[1])
        if i == 0:
            l1 = jnp.where(top_rows & (me < 2), 0.0, l1)
        g0 = l0 - dot3(split(l1), l0b)
        panel[0, part, :] = l0
        panel[1, part, :] = l1
        g = split(jnp.concatenate([g0, l1], axis=1))
        for ref, val in ((g_hi, g[0]), (g_lo, g[1])):
            ref[part, :] = lax.dot_general(
                val, order_t, (((1,), (1,)), ((), ())), preferred_element_type=jnp.float32
            ).astype(jnp.bfloat16)

    for copy in loads[2:]:
        copy.wait()
    flat = rows.reshape(2 * NT * DEV, NB)
    for c in range(DEV):
        hi, lo = split(flat[pl.ds(c, NT, stride=DEV), :])
        b_hi[:, c * NB : (c + 1) * NB] = hi
        b_lo[:, c * NB : (c + 1) * NB] = lo
    for copy in a_loads:
        copy.wait()
    fix_all(fix_row)

    aflat = a.reshape(ROWS * DEV, NB)
    stores = []
    for i in range(CHUNKS):
        part = pl.ds(i * CROWS, CROWS)

        for c in range(0, DEV, 2):
            wide = slice(c * NB, (c + 2) * NB)
            upd = dot3((g_hi[part, :], g_lo[part, :]), (b_hi[:, wide], b_lo[:, wide]))
            for h in range(2):
                where = pl.ds(i * CROWS * DEV + c + h, CROWS, stride=DEV)
                base = aflat[where, :]
                val = base - upd[:, h * NB : (h + 1) * NB]
                if c + h == 0:
                    fac = jnp.where(col == 0, panel[0, part, :], panel[1, part, :])
                    if i == 0:
                        top_rows = iota((CROWS, NB), 0) < NB
                        keep = jnp.where(col == 0, me == 0, me < 2)
                        same = top_rows & keep
                        base_or = jnp.where(col == 0, base, val)
                        fac = jnp.where(same, base_or, fac)
                    val = jnp.where(col < 2, fac, val)
                aflat[where, :] = val
        store = pltpu.make_async_copy(a.at[part], out_ref.at[part], sems.at[4 + i])
        store.start()
        stores.append(store)
    for store in stores:
        store.wait()


def update(table, inverses, work, new, old, panel, top):
    any_ = pl.BlockSpec(memory_space=pl.ANY)
    return pl.pallas_call(
        update_kernel,
        out_shape=jax.ShapeDtypeStruct((ROWS, DEV, NB), jnp.float32),
        in_specs=[
            pl.BlockSpec(memory_space=pltpu.SMEM),
            pl.BlockSpec(memory_space=pltpu.VMEM),
            pl.BlockSpec(memory_space=pltpu.VMEM),
            any_, any_, any_, any_, any_,
        ],
        out_specs=any_,
        scratch_shapes=[
            pltpu.VMEM((ROWS, DEV, NB), jnp.float32),
            pltpu.VMEM((2 * NT, DEV, NB), jnp.float32),
            pltpu.VMEM((2, ROWS, NB), jnp.float32),
            pltpu.VMEM((2, 2, NT, NB), jnp.float32),
            pltpu.VMEM((NT, DEV * NB), jnp.bfloat16),
            pltpu.VMEM((NT, DEV * NB), jnp.bfloat16),
            pltpu.VMEM((ROWS, NT), jnp.bfloat16),
            pltpu.VMEM((ROWS, NT), jnp.bfloat16),
            pltpu.SemaphoreType.DMA((4 + CHUNKS,)),
        ],
        compiler_params=pltpu.CompilerParams(vmem_limit_bytes=40 * MIB),
        name="update",
    )(table, inverses, table, work, new, old, panel, top)


def on_device(matrix, pivots, block_inverses):
    work = matrix.reshape(ROWS, DEV, NB)
    table, send = plan(pivots, work)

    def few():
        return move(FEW, table, send, work)

    def many():
        rows = jnp.take(work, table[T_SEND_MANY], axis=0)
        return move(MANY, table, rows, work)

    moved = lax.cond(table[T_MOST, 0] <= FEW * DEV, few, many)
    out = update(table, block_inverses, work, *moved)
    return out.reshape(matrix.shape)


def solution(mesh):
    in_specs = (P(None, "prow", None, None, "pcol", None), P(), P())
    out_specs = P(None, "prow", None, None, "pcol", None)
    return jax.shard_map(
        on_device, mesh=mesh, in_specs=in_specs, out_specs=out_specs, check_vma=False
    )
```

```python
import functools

import jax
import jax.numpy as jnp
from jax import lax
from jax.experimental import pallas as pl
from jax.experimental.pallas import tpu as pltpu
from jax.sharding import PartitionSpec as P

MESH = pl.DeviceIdType.MESH
NB = 128
NT = 256
DEV = 16
ROWS = 1024
FEW = 2
MANY = 16
OLD = {FEW: 2, MANY: 8}
MIB = 1 << 20

T_PLACE, T_FIX, T_COUNT, T_PICK, T_OUT, T_MID, T_MOST = range(7)


def iota(shape, dim):
    return lax.broadcasted_iota(jnp.int32, shape, dim)


def fiota(shape, dim):
    return iota(shape, dim).astype(jnp.float32)


def plan_kernel(k, piv_ref, a_ref, table_ref, send_ref, row_buf, row_smem, sem, row_sem):
    me = lax.axis_index("prow")
    old = OLD[k]
    sq = (NT, NT)
    sub, lane = fiota(sq, 0), fiota(sq, 1)
    diag = sub == lane
    lane1 = fiota((1, NT), 1)

    def to_col(row):
        row = row.astype(jnp.float32)
        return jnp.sum(jnp.where(diag, row, 0.0), axis=1, keepdims=True)

    def down(mask, value=1.0):
        return jnp.sum(jnp.where(mask, value, 0.0), axis=0, keepdims=True)

    def count(mask):
        return down(mask).astype(jnp.int32)

    def deal(cond, slot, value):
        slot_col = to_col(jnp.where(cond, slot, -1))
        return down(slot_col == lane, to_col(value)).astype(jnp.int32)

    def put(row, value):
        table_ref[row : row + 1, :] = jnp.broadcast_to(value, (1, NT)).astype(jnp.int32)

    piv = piv_ref[...].astype(jnp.float32)
    t_row = jnp.concatenate([piv[0:1, :], piv[1:2, :] + float(NB)], axis=1)
    t_col = to_col(t_row)
    before = sub < lane
    same = t_col == t_row
    last_same = jnp.max(jnp.where(same & before, sub, -1.0), axis=0, keepdims=True)
    later = jnp.max(jnp.where(same & (sub > lane), 1.0, 0.0), axis=0, keepdims=True)
    parent = jnp.max(jnp.where((t_col == lane) & before, sub, -1.0), axis=0, keepdims=True)
    c_row = jnp.where(parent < 0.0, lane1, parent)

    def jump(_, c_row):
        return down(sub == c_row, to_col(c_row))

    c_row = lax.fori_loop(0, 8, jump, c_row)

    from_swap = down(sub == last_same, to_col(c_row))
    src = jnp.where(last_same < 0.0, t_row, from_swap).astype(jnp.int32)
    owner = (src >> 7) & (DEV - 1)
    local = ((src >> 11) << 7) + (src & (NB - 1))
    owner_row, owner_col = owner.astype(jnp.float32), to_col(owner)
    less = owner_col < owner_row
    pos = count(less | ((owner_col == owner_row) & before))
    rank = pos - count(less)
    bin_, which = pos & (DEV - 1), rank >> 4
    send = deal((owner == me) & (which < k), bin_ * k + which, local)
    row_buf[0:1, :] = send
    to_smem = pltpu.make_async_copy(row_buf, row_smem, sem)
    to_smem.start()

    put(T_PLACE, bin_ * 16 + (pos >> 4))
    put(T_PICK, deal(bin_ == me, pos >> 4, owner * k + jnp.minimum(which, k - 1)))

    target, c = t_row.astype(jnp.int32), c_row.astype(jnp.int32)
    goes = (later < 0.5) & (target >= NT)
    to, block = (target >> 7) & (DEV - 1), c >> 7
    key = jnp.where(goes, block * DEV + to, 64)
    key_row, key_col = key.astype(jnp.float32), to_col(key)
    less = key_col < key_row
    pos = count(less | ((key_col == key_row) & before))
    rank_old = pos - count(less)
    pos = pos - count(key_col < (block * DEV).astype(jnp.float32))
    mid, slot, turn = pos & (DEV - 1), pos >> 4, rank_old >> 4
    fits = goes & (turn < old)
    put(T_OUT, deal(goes & (block == me), mid * 8 + slot, c & (NB - 1)))
    lane_of = block * old + turn
    put(T_MID, deal(fits & (mid == me), to * (2 * old) + lane_of, block * 8 + slot))
    mine = fits & (to == me)
    order = count(before & (to_col(jnp.where(mine, 1, 0)) > 0.5))
    dst = ((target >> 11) << 7) + (target & (NB - 1))
    put(T_FIX, deal(mine, order, dst * NT + mid * (2 * old) + lane_of))
    put(T_COUNT, jnp.sum(jnp.where(mine, 1.0, 0.0), axis=1, keepdims=True))
    most = jnp.maximum(rank, jnp.where(goes, rank_old, 0)).astype(jnp.float32)
    put(T_MOST, jnp.max(most, axis=1, keepdims=True))
    put(7, jnp.zeros((1, 1), jnp.int32))

    to_smem.wait()
    copies = [
        pltpu.make_async_copy(a_ref.at[row_smem[0, i]], send_ref.at[i], row_sem.at[i])
        for i in range(DEV * k)
    ]
    for copy in copies:
        copy.start()
    for copy in copies:
        copy.wait()


def plan(k, pivots, work):
    return pl.pallas_call(
        functools.partial(plan_kernel, k),
        out_shape=(
            jax.ShapeDtypeStruct((8, NT), jnp.int32),
            jax.ShapeDtypeStruct((DEV * k, DEV, NB), jnp.float32),
        ),
        in_specs=[pl.BlockSpec(memory_space=pltpu.VMEM), pl.BlockSpec(memory_space=pl.ANY)],
        out_specs=(pl.BlockSpec(memory_space=pltpu.VMEM), pl.BlockSpec(memory_space=pl.ANY)),
        scratch_shapes=[
            pltpu.VMEM((8, NT), jnp.int32),
            pltpu.SMEM((8, NT), jnp.int32),
            pltpu.SemaphoreType.DMA,
            pltpu.SemaphoreType.DMA((DEV * k,)),
        ],
        name=f"plan_{k}",
    )(pivots, work)


PIECES = 4


def move_kernel(
    k, table_ref, send_ref, a_ref,
    new_out, old_out, panel_out, top_out, side_out,
    got, mid, leave, leave2, first, new, old, panel, top, side,
    s_got, r_got, s_out, r_out, s_mid, r_mid, s_ag, r_ag, s_z, r_z, s_sib, r_sib,
    s_top, r_top, s_far, r_far, s_loc,
):
    me = lax.axis_index("prow")
    col = lax.axis_index("pcol")
    x, y = me // 4, me % 4
    z, core = col // 2, col % 2
    both = 2 * OLD[k]
    sends = []
    is_root, is_old = z == 0, me < 2

    def at(px, py):
        return (lax.rem(px + 4, 4) * 4 + lax.rem(py + 4, 4), col)

    def remote(src, dst, send_sem, recv_sem, device):
        return pltpu.make_async_remote_copy(
            src_ref=src, dst_ref=dst, send_sem=send_sem, recv_sem=recv_sem,
            device_id=device, device_id_type=MESH,
        )

    offsets = [(dx, dy) for dx in range(4) for dy in range(4) if (dx, dy) != (0, 0)]
    plane = [at(x + dx, y + dy) for dx, dy in offsets]
    origin = [at(x - dx, y - dy) for dx, dy in offsets]
    sibling = (me, z * 2 + 1 - core)
    others = [(me, lax.rem(z + i, 4) * 2 + core) for i in (1, 2, 3)]

    mine = pltpu.make_async_copy(a_ref.at[:, 0, :], panel.at[core], s_loc.at[0])
    block = pltpu.make_async_copy(a_ref.at[pl.ds(0, NB)], first, s_loc.at[1])

    @pl.when(is_root)
    def _():
        mine.start()

    @pl.when(is_old)
    def _():
        block.start()

    barrier = pltpu.get_barrier_semaphore()
    greeted = plane + others + [sibling]
    for device in greeted:
        pl.semaphore_signal(barrier, inc=1, device_id=device, device_id_type=MESH)

    @pl.when(is_old)
    def _():
        block.wait()

        @pl.loop(0, NB)
        def _(i):
            leave[i] = first[table_ref[T_OUT, i]]

    pl.semaphore_wait(barrier, len(greeted))

    def exchange(src, dst, n, s_sem, r_sem):
        for j, device in enumerate(plane):
            copy = remote(
                src.at[pl.ds(device[0] * n, n)], dst.at[pl.ds(me * n, n)],
                s_sem.at[j], r_sem.at[j], device,
            )
            copy.start()
            sends.append(copy)

    def exchanged(src, dst, n, s_sem, r_sem):
        for j, device in enumerate(origin):
            remote(
                src.at[pl.ds(0, n)], dst.at[pl.ds(device[0] * n, n)],
                s_sem.at[j], r_sem.at[j], device,
            ).wait_recv()

    exchange(send_ref, got, k, s_got, r_got)
    own = pltpu.make_async_copy(
        send_ref.at[pl.ds(me * k, k)], got.at[pl.ds(me * k, k)], s_loc.at[2]
    )
    own.start()

    stage = jnp.where(core == 0, z, lax.rem(4 - z, 4))
    onward = (me, jnp.where(core == 0, lax.rem(z + 1, 4), lax.rem(z + 3, 4)) * 2 + core)
    size = ROWS // PIECES

    def z_part(i):
        return panel.at[core, pl.ds(i * size, size)]

    def z_onward(i):
        return remote(z_part(i), z_part(i), s_z.at[i], r_z.at[i], onward)

    def z_sibling(i):
        return remote(z_part(i), z_part(i), s_sib.at[i], r_sib.at[i], sibling)

    def z_step(i):
        @pl.when(z > 0)
        def _():
            z_onward(i).wait_recv()

            @pl.when(stage < 3)
            def _():
                z_onward(i).start()

            z_sibling(i).start()

    def z_finish(i):
        @pl.when(stage < 3)
        def _():
            z_onward(i).wait_send()

        z_sibling(i).wait_send()
        part = panel.at[1 - core, pl.ds(i * size, size)]
        remote(part, part, s_sib.at[i], r_sib.at[i], sibling).wait_recv()

    @pl.when(is_root)
    def _():
        mine.wait()
        for i in range(PIECES):
            z_onward(i).start()
            z_sibling(i).start()

    def deal_out(half):
        return [
            remote(
                leave.at[pl.ds(device[0] * 8, 8)], mid.at[pl.ds(half * 8, 8)],
                s_out.at[j], r_out.at[half], device,
            )
            for j, device in enumerate(plane)
        ]

    def deal_own(half):
        return pltpu.make_async_copy(
            leave.at[pl.ds(me * 8, 8)], mid.at[pl.ds(half * 8, 8)], s_loc.at[3]
        )

    for half in range(2):

        @pl.when(me == half)
        def _():
            deal_own(half).start()
            for copy in deal_out(half):
                copy.start()

    def ring(axis, step):
        if axis == 0:
            return lax.rem(x + step + 4, 4) * 4 + y
        return x * 4 + lax.rem(y + step + 4, 4)

    def shifted(index, axis, step):
        px, py = index // 4, index % 4
        if axis == 0:
            return lax.rem(px + step + 4, 4) * 4 + py
        return px * 4 + lax.rem(py + step + 4, 4)

    def part_of(index, half, part=None):
        if part is None:
            return new.at[pl.ds(index * 16, 16), pl.ds(half * 8, 8)]
        return new.at[pl.ds(index * 16 + part * 8, 8), pl.ds(half * 8, 8)]

    class Gather:
        def __init__(self, half):
            self.half, self.base = half, half * 20
            self.axes = (0, 1) if half == 0 else (1, 0)

        def copy(self, phase, item, role, index, part=None):
            n = self.base + phase * (1 + item) * 4 + role
            ref = part_of(index, self.half, part)
            device = (ring(self.axes[phase], 1 if role % 2 == 0 else 3), col)
            return remote(ref, ref, s_ag.at[n], r_ag.at[n], device)

        def send(self, *args):
            copy = self.copy(*args)
            copy.start()
            sends.append(copy)

        def start(self, phase, item, index):
            for role in range(2):
                self.send(phase, item, role, index)

        def near(self, phase, item, index, role):
            came = shifted(index, self.axes[phase], 3 if role == 0 else 1)
            self.copy(phase, item, role, came).wait_recv()
            self.send(phase, item, 2 + role, came, role)
            return came

        def far(self, phase, item, index):
            came = shifted(index, self.axes[phase], 2)
            for role in range(2):
                self.copy(phase, item, 2 + role, came, role).wait_recv()
            return came

    exchanged(send_ref, got, k, s_got, r_got)
    own.wait()
    for i in range(16):
        new[me * 16 + i] = got[table_ref[T_PICK, i]]
    halves = [Gather(h) for h in range(2)]
    items = [[me], [me]]
    for g in halves:
        g.start(0, 0, me)
    for g in halves:
        g.start(1, 0, me)

    def top_part(index):
        return top.at[core, pl.ds(index * 16, 16)]

    def top_send(j):
        return remote(top_part(me), top_part(me), s_top.at[j], r_top.at[j], plane[j])

    def spread(kind, i):
        ref = (top if kind == 0 else side).at[core]
        return remote(ref, ref, s_far.at[kind, i], r_far.at[kind], others[i])

    def pass_on(kind):
        ref = (top if kind == 0 else side).at[core]
        n = PIECES + kind
        return remote(ref, ref, s_sib.at[n], r_sib.at[n], sibling)

    def from_sibling(kind):
        ref = (top if kind == 0 else side).at[1 - core]
        n = PIECES + kind
        return remote(ref, ref, s_sib.at[n], r_sib.at[n], sibling)

    @pl.when(is_root)
    def _():
        top[core, pl.ds(me * 16, 16), :] = new.reshape(NT * DEV, NB)[
            pl.ds(me * 16 * DEV, 16, stride=DEV), :
        ]
        for j in range(len(plane)):
            top_send(j).start()

    z_step(0)

    for half in range(2):

        @pl.when(me == half)
        def _():
            deal_own(half).wait()

        @pl.when(me != half)
        def _():
            ref = mid.at[pl.ds(half * 8, 8)]
            remote(ref, ref, s_out.at[0], r_out.at[half], plane[0]).wait_recv()

    for i in range(DEV * both):
        leave2[i] = mid[table_ref[T_MID, i]]
    exchange(leave2, old, both, s_mid, r_mid)
    own_old = pltpu.make_async_copy(
        leave2.at[pl.ds(me * both, both)], old.at[pl.ds(me * both, both)], s_loc.at[4]
    )
    own_old.start()

    z_step(1)
    for role in range(2):
        for h, g in enumerate(halves):
            came = g.near(0, 0, me, role)
            g.start(1, 1 + role, came)
            items[h].append(came)
    z_step(2)
    for h, g in enumerate(halves):
        came = g.far(0, 0, me)
        g.start(1, 3, came)
        items[h].append(came)
    z_step(3)

    @pl.when(is_root)
    def _():
        for j in range(len(plane)):
            index = origin[j][0]
            remote(
                top_part(index), top_part(index), s_top.at[j], r_top.at[j], plane[j]
            ).wait_recv()
        for i in range(3):
            spread(0, i).start()
        pass_on(0).start()

    def forward(i):
        for h, g in enumerate(halves):
            for role in range(2):
                g.near(1, i, items[h][i], role)

    forward(0)
    forward(1)

    @pl.when(z > 0)
    def _():
        spread(0, 0).wait_recv()
        pass_on(0).start()

    forward(2)
    forward(3)
    exchanged(leave2, old, both, s_mid, r_mid)
    own_old.wait()

    @pl.when(is_root)
    def _():
        side[core] = old.reshape(DEV * both * DEV, NB)[
            pl.ds(0, DEV * both, stride=DEV), :
        ]
        for i in range(3):
            spread(1, i).start()
        pass_on(1).start()

    def out(i, src, dst):
        return pltpu.make_async_copy(src, dst, s_loc.at[5 + i])

    outs = [out(0, old, old_out)]
    outs[0].start()
    for i in range(PIECES):
        z_finish(i)
    outs.append(out(1, panel, panel_out))
    outs[1].start()
    for i in range(4):
        for h, g in enumerate(halves):
            g.far(1, i, items[h][i])
    outs.append(out(2, new, new_out))
    outs[2].start()

    @pl.when(z > 0)
    def _():
        spread(1, 0).wait_recv()
        pass_on(1).start()

    for kind in range(2):
        from_sibling(kind).wait_recv()
    outs.append(out(3, top, top_out))
    outs.append(out(4, side, side_out))
    outs[3].start()
    outs[4].start()
    for kind in range(2):
        pass_on(kind).wait_send()

    @pl.when(is_root)
    def _():
        for kind in range(2):
            for i in range(3):
                spread(kind, i).wait_send()
        for j in range(len(plane)):
            top_send(j).wait_send()

    for half in range(2):

        @pl.when(me == half)
        def _():
            for copy in deal_out(half):
                copy.wait_send()

    for copy in sends:
        copy.wait_send()
    for copy in outs:
        copy.wait()


def move(k, table, send, work):
    both = 2 * OLD[k]
    outs = (
        (NT, DEV, NB),
        (DEV * both, DEV, NB),
        (2, ROWS, NB),
        (2, NT, NB),
        (2, DEV * both, NB),
    )
    dma = pltpu.SemaphoreType.DMA
    scratch = ((DEV * k, DEV, NB), (16, DEV, NB), (NB, DEV, NB), outs[1], (NB, DEV, NB)) + outs
    return pl.pallas_call(
        functools.partial(move_kernel, k),
        out_shape=tuple(jax.ShapeDtypeStruct(s, jnp.float32) for s in outs),
        in_specs=[
            pl.BlockSpec(memory_space=pltpu.SMEM),
            pl.BlockSpec(memory_space=pl.ANY),
            pl.BlockSpec(memory_space=pl.ANY),
        ],
        out_specs=tuple(pl.BlockSpec(memory_space=pl.ANY) for _ in outs),
        scratch_shapes=[pltpu.VMEM(s, jnp.float32) for s in scratch]
        + [
            dma((15,)), dma((15,)), dma((15,)), dma((2,)), dma((15,)), dma((15,)),
            dma((40,)), dma((40,)), dma((PIECES,)), dma((PIECES,)),
            dma((PIECES + 2,)), dma((PIECES + 2,)), dma((15,)), dma((15,)),
            dma((2, 3)), dma((2,)), dma((10,)),
        ],
        compiler_params=pltpu.CompilerParams(
            collective_id=k, has_side_effects=True, vmem_limit_bytes=24 * MIB
        ),
        name=f"move_{k}",
    )(table, send, work)


def split(a):
    hi = a.astype(jnp.bfloat16)
    return hi, (a - hi.astype(jnp.float32)).astype(jnp.bfloat16)


def dot(a, b):
    return jnp.dot(a, b, preferred_element_type=jnp.float32)


def dot3(a, b):
    return dot(a[0], b[0]) + (dot(a[0], b[1]) + dot(a[1], b[0]))


CHUNKS = 4
CROWS = ROWS // CHUNKS


def update_kernel(
    n_old, table_ref, inv_ref, place_ref, a_ref, new_ref, old_ref, panel_ref, top_ref, side_ref,
    out_ref,
    a, rows, panel, top, b_hi, b_lo, g_hi, g_lo, sems,
):
    me = lax.axis_index("prow")
    col = lax.axis_index("pcol")
    loads = [
        pltpu.make_async_copy(panel_ref, panel, sems.at[0]),
        pltpu.make_async_copy(top_ref, top.at[:, pl.ds(0, NT)], sems.at[1]),
        pltpu.make_async_copy(side_ref, top.at[:, pl.ds(NT, n_old)], sems.at[2]),
        pltpu.make_async_copy(new_ref, rows.at[pl.ds(0, NT)], sems.at[3]),
        pltpu.make_async_copy(old_ref, rows.at[pl.ds(NT, n_old)], sems.at[4]),
    ]
    a_loads = [
        pltpu.make_async_copy(
            a_ref.at[pl.ds(i * CROWS, CROWS)], a.at[pl.ds(i * CROWS, CROWS)], sems.at[5 + i]
        )
        for i in range(CHUNKS)
    ]
    for copy in loads + a_loads:
        copy.start()
    for copy in loads[:3]:
        copy.wait()

    count = table_ref[T_COUNT, 0]

    def fix_panel(dst, src):
        for p in range(2):
            panel[p, pl.ds(dst, 1), :] = top[p, pl.ds(src, 1), :]

    def fix_row(dst, src):
        a[dst] = rows[src]

    def fix_all(fix):
        @pl.when(me < 2)
        def _():
            @pl.loop(0, NB)
            def _(i):
                fix(i, table_ref[T_PLACE, me * NB + i])

        @pl.loop(0, count)
        def _(i):
            entry = table_ref[T_FIX, i]
            fix(entry >> 8, NT + (entry & (NT - 1)))

    fix_all(fix_panel)

    place = place_ref[T_PLACE : T_PLACE + 1, :]
    order_t = jnp.where(iota((NT, NT), 0) == place, 1.0, 0.0).astype(jnp.bfloat16)

    def pick(lo, val):
        return lax.dot_general(
            order_t[:, lo : lo + NB], val, (((0,), (0,)), ((), ())),
            preferred_element_type=jnp.float32,
        )

    inv = [split(inv_ref[s]) for s in range(2)]
    u_split = split(top[1, 0:NT, :])
    u0p = tuple(pick(0, v).astype(jnp.bfloat16) for v in u_split)
    p_split = split(top[0, 0:NT, :])
    l0b = dot3(tuple(pick(NB, v).astype(jnp.bfloat16) for v in p_split), inv[0])
    l0b = split(l0b)

    for i in range(CHUNKS):
        part = pl.ds(i * CROWS, CROWS)
        l0 = dot3(split(panel[0, part, :]), inv[0])
        if i == 0:
            top_rows = iota((CROWS, NB), 0) < NB
            l0 = jnp.where(top_rows & (me == 0), 0.0, l0)
        rest = panel[1, part, :] - dot3(split(l0), u0p)
        l1 = dot3(split(rest), inv[1])
        if i == 0:
            l1 = jnp.where(top_rows & (me < 2), 0.0, l1)
        g0 = l0 - dot3(split(l1), l0b)
        panel[0, part, :] = l0
        panel[1, part, :] = l1
        g = split(jnp.concatenate([g0, l1], axis=1))
        for ref, val in ((g_hi, g[0]), (g_lo, g[1])):
            ref[part, :] = lax.dot_general(
                val, order_t, (((1,), (1,)), ((), ())), preferred_element_type=jnp.float32
            ).astype(jnp.bfloat16)

    for copy in loads[3:]:
        copy.wait()
    flat = rows.reshape((NT + n_old) * DEV, NB)
    for c in range(DEV):
        hi, lo = split(flat[pl.ds(c, NT, stride=DEV), :])
        b_hi[:, c * NB : (c + 1) * NB] = hi
        b_lo[:, c * NB : (c + 1) * NB] = lo
    for copy in a_loads:
        copy.wait()
    fix_all(fix_row)

    aflat = a.reshape(ROWS * DEV, NB)
    stores = []
    for i in range(CHUNKS):
        part = pl.ds(i * CROWS, CROWS)

        for c in range(0, DEV, 2):
            wide = slice(c * NB, (c + 2) * NB)
            upd = dot3((g_hi[part, :], g_lo[part, :]), (b_hi[:, wide], b_lo[:, wide]))
            for h in range(2):
                where = pl.ds(i * CROWS * DEV + c + h, CROWS, stride=DEV)
                base = aflat[where, :]
                val = base - upd[:, h * NB : (h + 1) * NB]
                if c + h == 0:
                    fac = jnp.where(col == 0, panel[0, part, :], panel[1, part, :])
                    if i == 0:
                        top_rows = iota((CROWS, NB), 0) < NB
                        keep = jnp.where(col == 0, me == 0, me < 2)
                        same = top_rows & keep
                        base_or = jnp.where(col == 0, base, val)
                        fac = jnp.where(same, base_or, fac)
                    val = jnp.where(col < 2, fac, val)
                aflat[where, :] = val
        store = pltpu.make_async_copy(a.at[part], out_ref.at[part], sems.at[5 + i])
        store.start()
        stores.append(store)
    for store in stores:
        store.wait()


def update(table, inverses, work, new, old, panel, top, side):
    n_old = old.shape[0]
    any_ = pl.BlockSpec(memory_space=pl.ANY)
    return pl.pallas_call(
        functools.partial(update_kernel, n_old),
        out_shape=jax.ShapeDtypeStruct((ROWS, DEV, NB), jnp.float32),
        in_specs=[
            pl.BlockSpec(memory_space=pltpu.SMEM),
            pl.BlockSpec(memory_space=pltpu.VMEM),
            pl.BlockSpec(memory_space=pltpu.VMEM),
            any_, any_, any_, any_, any_, any_,
        ],
        out_specs=any_,
        scratch_shapes=[
            pltpu.VMEM((ROWS, DEV, NB), jnp.float32),
            pltpu.VMEM((NT + n_old, DEV, NB), jnp.float32),
            pltpu.VMEM((2, ROWS, NB), jnp.float32),
            pltpu.VMEM((2, NT + n_old, NB), jnp.float32),
            pltpu.VMEM((NT, DEV * NB), jnp.bfloat16),
            pltpu.VMEM((NT, DEV * NB), jnp.bfloat16),
            pltpu.VMEM((ROWS, NT), jnp.bfloat16),
            pltpu.VMEM((ROWS, NT), jnp.bfloat16),
            pltpu.SemaphoreType.DMA((5 + CHUNKS,)),
        ],
        compiler_params=pltpu.CompilerParams(vmem_limit_bytes=40 * MIB),
        name=f"update_{n_old}",
    )(table, inverses, table, work, new, old, panel, top, side)


def on_device(matrix, pivots, block_inverses):
    work = matrix.reshape(ROWS, DEV, NB)
    table, send = plan(FEW, pivots, work)

    def few():
        return update(table, block_inverses, work, *move(FEW, table, send, work))

    def many():
        table, send = plan(MANY, pivots, work)
        return update(table, block_inverses, work, *move(MANY, table, send, work))

    out = lax.cond(table[T_MOST, 0] < FEW * DEV, few, many)
    return out.reshape(matrix.shape)


def solution(mesh):
    in_specs = (P(None, "prow", None, None, "pcol", None), P(), P())
    out_specs = P(None, "prow", None, None, "pcol", None)
    return jax.shard_map(
        on_device, mesh=mesh, in_specs=in_specs, out_specs=out_specs, check_vma=False
    )
```

```python
import functools

import jax
import jax.numpy as jnp
from jax import lax
from jax.experimental import pallas as pl
from jax.experimental.pallas import tpu as pltpu
from jax.sharding import PartitionSpec as P

MESH = pl.DeviceIdType.MESH
NB = 128
NT = 256
DEV = 16
ROWS = 1024
FEW = 2
MANY = 16
OLD = {FEW: 3, MANY: 16}
N_OLD = {k: DEV * n for k, n in OLD.items()}
MIB = 1 << 20

T_PLACE, T_FIX, T_COUNT, T_PICK, T_OUT, T_MID, T_OVER = range(7)


def iota(shape, dim):
    return lax.broadcasted_iota(jnp.int32, shape, dim)


def fiota(shape, dim):
    return iota(shape, dim).astype(jnp.float32)


def plan_kernel(k, piv_ref, a_ref, table_ref, send_ref, row_buf, row_smem, sem, row_sem):
    me = lax.axis_index("prow")
    old = OLD[k]
    sq = (NT, NT)
    sub, lane = fiota(sq, 0), fiota(sq, 1)
    diag = sub == lane
    lane1 = fiota((1, NT), 1)

    def to_col(row):
        row = row.astype(jnp.float32)
        return jnp.sum(jnp.where(diag, row, 0.0), axis=1, keepdims=True)

    def down(mask, value=1.0):
        return jnp.sum(jnp.where(mask, value, 0.0), axis=0, keepdims=True)

    def count(mask):
        return down(mask).astype(jnp.int32)

    def deal(cond, slot, value):
        slot_col = to_col(jnp.where(cond, slot, -1))
        return down(slot_col == lane, to_col(value)).astype(jnp.int32)

    def put(row, value):
        table_ref[row : row + 1, :] = jnp.broadcast_to(value, (1, NT)).astype(jnp.int32)

    piv = piv_ref[...].astype(jnp.float32)
    t_row = jnp.concatenate([piv[0:1, :], piv[1:2, :] + float(NB)], axis=1)
    t_col = to_col(t_row)
    before = sub < lane
    same = t_col == t_row
    last_same = jnp.max(jnp.where(same & before, sub, -1.0), axis=0, keepdims=True)
    later = jnp.max(jnp.where(same & (sub > lane), 1.0, 0.0), axis=0, keepdims=True)
    parent = jnp.max(jnp.where((t_col == lane) & before, sub, -1.0), axis=0, keepdims=True)
    c_row = jnp.where(parent < 0.0, lane1, parent)

    def jump(_, c_row):
        return down(sub == c_row, to_col(c_row))

    c_row = lax.fori_loop(0, 8, jump, c_row)

    from_swap = down(sub == last_same, to_col(c_row))
    src = jnp.where(last_same < 0.0, t_row, from_swap).astype(jnp.int32)
    owner = (src >> 7) & (DEV - 1)
    local = ((src >> 11) << 7) + (src & (NB - 1))
    owner_row, owner_col = owner.astype(jnp.float32), to_col(owner)
    less = owner_col < owner_row
    pos = count(less | ((owner_col == owner_row) & before))
    rank = pos - count(less)
    bin_, which = pos & (DEV - 1), rank >> 4
    send = deal((owner == me) & (which < k), bin_ * k + which, local)
    row_buf[0:1, :] = send
    to_smem = pltpu.make_async_copy(row_buf, row_smem, sem)
    to_smem.start()

    put(T_PLACE, bin_ * 16 + (pos >> 4))
    put(T_PICK, deal(bin_ == me, pos >> 4, owner * k + jnp.minimum(which, k - 1)))

    target, c = t_row.astype(jnp.int32), c_row.astype(jnp.int32)
    goes = (later < 0.5) & (target >= NT)
    to, block = (target >> 7) & (DEV - 1), c >> 7
    key = jnp.where(goes, block * DEV + to, 64)
    key_row, key_col = key.astype(jnp.float32), to_col(key)
    less = key_col < key_row
    pos = count(less | ((key_col == key_row) & before))
    pos = pos - count(key_col < (block * DEV).astype(jnp.float32))
    mid, slot = pos & (DEV - 1), pos >> 4
    pair = jnp.where(goes, to * DEV + mid, NT)
    turn = count((to_col(pair) == pair.astype(jnp.float32)) & before)
    put(T_OUT, deal(goes & (block == me), mid * 8 + slot, c & (NB - 1)))
    put(T_MID, deal(goes & (turn < old) & (mid == me), to * old + turn, block * 8 + slot))
    mine = goes & (to == me)
    order = count(before & (to_col(jnp.where(mine, 1, 0)) > 0.5))
    dst = ((target >> 11) << 7) + (target & (NB - 1))
    put(T_FIX, deal(mine, order, dst * NT + mid * DEV + turn))
    put(T_COUNT, jnp.sum(jnp.where(mine, 1.0, 0.0), axis=1, keepdims=True))
    over = (which >= k) | (goes & (turn >= old))
    put(T_OVER, jnp.max(jnp.where(over, 1.0, 0.0), axis=1, keepdims=True))
    put(7, jnp.zeros((1, 1), jnp.int32))

    to_smem.wait()
    copies = [
        pltpu.make_async_copy(a_ref.at[row_smem[0, i]], send_ref.at[i], row_sem.at[i])
        for i in range(DEV * k)
    ]
    for copy in copies:
        copy.start()
    for copy in copies:
        copy.wait()


def plan(k, pivots, work):
    return pl.pallas_call(
        functools.partial(plan_kernel, k),
        out_shape=(
            jax.ShapeDtypeStruct((8, NT), jnp.int32),
            jax.ShapeDtypeStruct((DEV * k, DEV, NB), jnp.float32),
        ),
        in_specs=[pl.BlockSpec(memory_space=pltpu.VMEM), pl.BlockSpec(memory_space=pl.ANY)],
        out_specs=(pl.BlockSpec(memory_space=pltpu.VMEM), pl.BlockSpec(memory_space=pl.ANY)),
        scratch_shapes=[
            pltpu.VMEM((8, NT), jnp.int32),
            pltpu.SMEM((8, NT), jnp.int32),
            pltpu.SemaphoreType.DMA,
            pltpu.SemaphoreType.DMA((DEV * k,)),
        ],
        name=f"plan_{k}",
    )(pivots, work)


def split(a):
    hi = a.astype(jnp.bfloat16)
    return hi, (a - hi.astype(jnp.float32)).astype(jnp.bfloat16)


def dot(a, b):
    return jnp.dot(a, b, preferred_element_type=jnp.float32)


def dot3(a, b):
    return dot(a[0], b[0]) + (dot(a[0], b[1]) + dot(a[1], b[0]))


PIECES = 4


def move_kernel(
    k, table_ref, place_ref, inv_ref, send_ref, a_ref,
    new, old, g_ref, fac_ref, side_g,
    got, mid, leave, leave2, first, panel, top, side,
    s_got, r_got, s_out, r_out, s_mid, r_mid, s_ag, r_ag, s_z, r_z, s_sib, r_sib,
    s_top, r_top, s_far, r_far, s_loc,
):
    me = lax.axis_index("prow")
    col = lax.axis_index("pcol")
    x, y = me // 4, me % 4
    z, core = col // 2, col % 2
    both = OLD[k]
    sends = []
    is_root, is_old = z == 0, me < 2

    def at(px, py):
        return (lax.rem(px + 4, 4) * 4 + lax.rem(py + 4, 4), col)

    def remote(src, dst, send_sem, recv_sem, device):
        return pltpu.make_async_remote_copy(
            src_ref=src, dst_ref=dst, send_sem=send_sem, recv_sem=recv_sem,
            device_id=device, device_id_type=MESH,
        )

    offsets = [(dx, dy) for dx in range(4) for dy in range(4) if (dx, dy) != (0, 0)]
    plane = [at(x + dx, y + dy) for dx, dy in offsets]
    origin = [at(x - dx, y - dy) for dx, dy in offsets]
    sibling = (me, z * 2 + 1 - core)
    others = [(me, lax.rem(z + i, 4) * 2 + core) for i in (1, 2, 3)]

    mine = pltpu.make_async_copy(a_ref.at[:, 0, :], panel.at[core], s_loc.at[0])
    block = pltpu.make_async_copy(a_ref.at[pl.ds(0, NB)], first, s_loc.at[1])

    @pl.when(is_root)
    def _():
        mine.start()

    @pl.when(is_old)
    def _():
        block.start()

    barrier = pltpu.get_barrier_semaphore()
    greeted = plane + others + [sibling]
    for device in greeted:
        pl.semaphore_signal(barrier, inc=1, device_id=device, device_id_type=MESH)

    @pl.when(is_old)
    def _():
        block.wait()

        @pl.loop(0, NB)
        def _(i):
            leave[i] = first[table_ref[T_OUT, i]]

    pl.semaphore_wait(barrier, len(greeted))

    def exchange(src, dst, n, s_sem, r_sem):
        for j, device in enumerate(plane):
            copy = remote(
                src.at[pl.ds(device[0] * n, n)], dst.at[pl.ds(me * n, n)],
                s_sem.at[j], r_sem.at[j], device,
            )
            copy.start()
            sends.append(copy)

    def exchanged(src, dst, n, s_sem, r_sem):
        for j, device in enumerate(origin):
            remote(
                src.at[pl.ds(0, n)], dst.at[pl.ds(device[0] * n, n)],
                s_sem.at[j], r_sem.at[j], device,
            ).wait_recv()

    exchange(send_ref, got, k, s_got, r_got)
    own = pltpu.make_async_copy(
        send_ref.at[pl.ds(me * k, k)], got.at[pl.ds(me * k, k)], s_loc.at[2]
    )
    own.start()

    stage = jnp.where(core == 0, z, lax.rem(4 - z, 4))
    onward = (me, jnp.where(core == 0, lax.rem(z + 1, 4), lax.rem(z + 3, 4)) * 2 + core)
    size = ROWS // PIECES

    def z_part(i):
        return panel.at[core, pl.ds(i * size, size)]

    def z_onward(i):
        return remote(z_part(i), z_part(i), s_z.at[i], r_z.at[i], onward)

    def z_sibling(i):
        return remote(z_part(i), z_part(i), s_sib.at[i], r_sib.at[i], sibling)

    def z_step(i):
        @pl.when(z > 0)
        def _():
            z_onward(i).wait_recv()

            @pl.when(stage < 3)
            def _():
                z_onward(i).start()

            z_sibling(i).start()

    def z_finish(i):
        @pl.when(stage < 3)
        def _():
            z_onward(i).wait_send()

        z_sibling(i).wait_send()
        part = panel.at[1 - core, pl.ds(i * size, size)]
        remote(part, part, s_sib.at[i], r_sib.at[i], sibling).wait_recv()

    @pl.when(is_root)
    def _():
        mine.wait()
        for i in range(PIECES):
            z_onward(i).start()
            z_sibling(i).start()

    def deal_out(half):
        return [
            remote(
                leave.at[pl.ds(device[0] * 8, 8)], mid.at[pl.ds(half * 8, 8)],
                s_out.at[j], r_out.at[half], device,
            )
            for j, device in enumerate(plane)
        ]

    def deal_own(half):
        return pltpu.make_async_copy(
            leave.at[pl.ds(me * 8, 8)], mid.at[pl.ds(half * 8, 8)], s_loc.at[3]
        )

    for half in range(2):

        @pl.when(me == half)
        def _():
            deal_own(half).start()
            for copy in deal_out(half):
                copy.start()

    def ring(axis, step):
        if axis == 0:
            return lax.rem(x + step + 4, 4) * 4 + y
        return x * 4 + lax.rem(y + step + 4, 4)

    def shifted(index, axis, step):
        px, py = index // 4, index % 4
        if axis == 0:
            return lax.rem(px + step + 4, 4) * 4 + py
        return px * 4 + lax.rem(py + step + 4, 4)

    def part_of(index, half, part=None):
        if part is None:
            return new.at[pl.ds(index * 16, 16), pl.ds(half * 8, 8)]
        return new.at[pl.ds(index * 16 + part * 8, 8), pl.ds(half * 8, 8)]

    class Gather:
        def __init__(self, half):
            self.half, self.base = half, half * 20
            self.axes = (0, 1) if half == 0 else (1, 0)

        def copy(self, phase, item, role, index, part=None):
            n = self.base + phase * (1 + item) * 4 + role
            ref = part_of(index, self.half, part)
            device = (ring(self.axes[phase], 1 if role % 2 == 0 else 3), col)
            return remote(ref, ref, s_ag.at[n], r_ag.at[n], device)

        def send(self, *args):
            copy = self.copy(*args)
            copy.start()
            sends.append(copy)

        def start(self, phase, item, index):
            for role in range(2):
                self.send(phase, item, role, index)

        def near(self, phase, item, index, role):
            came = shifted(index, self.axes[phase], 3 if role == 0 else 1)
            self.copy(phase, item, role, came).wait_recv()
            self.send(phase, item, 2 + role, came, role)
            return came

        def far(self, phase, item, index):
            came = shifted(index, self.axes[phase], 2)
            for role in range(2):
                self.copy(phase, item, 2 + role, came, role).wait_recv()
            return came

    exchanged(send_ref, got, k, s_got, r_got)
    own.wait()
    for i in range(16):
        new[me * 16 + i] = got[table_ref[T_PICK, i]]
    halves = [Gather(h) for h in range(2)]
    items = [[me], [me]]
    for g in halves:
        g.start(0, 0, me)
    for g in halves:
        g.start(1, 0, me)

    def top_part(index):
        return top.at[core, pl.ds(index * 16, 16)]

    def top_send(j):
        return remote(top_part(me), top_part(me), s_top.at[j], r_top.at[j], plane[j])

    def spread(kind, i):
        ref = (top if kind == 0 else side).at[core]
        return remote(ref, ref, s_far.at[kind, i], r_far.at[kind], others[i])

    def pass_on(kind):
        ref = (top if kind == 0 else side).at[core]
        n = PIECES + kind
        return remote(ref, ref, s_sib.at[n], r_sib.at[n], sibling)

    def from_sibling(kind):
        ref = (top if kind == 0 else side).at[1 - core]
        n = PIECES + kind
        return remote(ref, ref, s_sib.at[n], r_sib.at[n], sibling)

    @pl.when(is_root)
    def _():
        top[core, pl.ds(me * 16, 16), :] = new.reshape(NT * DEV, NB)[
            pl.ds(me * 16 * DEV, 16, stride=DEV), :
        ]
        for j in range(len(plane)):
            top_send(j).start()

    z_step(0)
    for role in range(2):
        for h, g in enumerate(halves):
            came = g.near(0, 0, me, role)
            g.start(1, 1 + role, came)
            items[h].append(came)
    z_step(1)
    for h, g in enumerate(halves):
        came = g.far(0, 0, me)
        g.start(1, 3, came)
        items[h].append(came)

    for half in range(2):

        @pl.when(me == half)
        def _():
            deal_own(half).wait()

        @pl.when(me != half)
        def _():
            ref = mid.at[pl.ds(half * 8, 8)]
            remote(ref, ref, s_out.at[0], r_out.at[half], plane[0]).wait_recv()

    for i in range(DEV * both):
        leave2[i] = mid[table_ref[T_MID, i]]
    exchange(leave2, old, both, s_mid, r_mid)
    own_old = pltpu.make_async_copy(
        leave2.at[pl.ds(me * both, both)], old.at[pl.ds(me * both, both)], s_loc.at[4]
    )
    own_old.start()

    z_step(2)
    z_step(3)

    @pl.when(is_root)
    def _():
        for j in range(len(plane)):
            index = origin[j][0]
            remote(
                top_part(index), top_part(index), s_top.at[j], r_top.at[j], plane[j]
            ).wait_recv()
        for i in range(3):
            spread(0, i).start()
        pass_on(0).start()

    def forward(i):
        for h, g in enumerate(halves):
            for role in range(2):
                g.near(1, i, items[h][i], role)

    forward(0)
    forward(1)

    @pl.when(z > 0)
    def _():
        spread(0, 0).wait_recv()
        pass_on(0).start()

    forward(2)
    forward(3)
    exchanged(leave2, old, both, s_mid, r_mid)
    own_old.wait()

    @pl.when(is_root)
    def _():
        side[core] = old.reshape(N_OLD[MANY] * DEV, NB)[pl.ds(0, DEV * both, stride=DEV), :]
        for i in range(3):
            spread(1, i).start()
        pass_on(1).start()

    for i in range(PIECES):
        z_finish(i)
    from_sibling(0).wait_recv()

    place = place_ref[T_PLACE : T_PLACE + 1, :]
    order_t = jnp.where(iota((NT, NT), 0) == place, 1.0, 0.0).astype(jnp.bfloat16)

    def pick(lo, val):
        return lax.dot_general(
            order_t[:, lo : lo + NB], val, (((0,), (0,)), ((), ())),
            preferred_element_type=jnp.float32,
        ).astype(jnp.bfloat16)

    inv = [split(inv_ref[s]) for s in range(2)]
    u0p = tuple(pick(0, v) for v in split(top[1]))
    l0b_full = dot3(tuple(pick(NB, v) for v in split(top[0])), inv[0])
    l0b = split(l0b_full)

    def factors(p0, p1):
        l0 = dot3(split(p0), inv[0])
        l1 = dot3(split(p1 - dot3(split(l0), u0p)), inv[1])
        return l0, l0 - dot3(split(l1), l0b), l1

    for i in range(4):
        part = pl.ds(i * 256, 256)
        l0, g0, l1 = factors(panel[0, part, :], panel[1, part, :])
        fac_ref[part, :] = l0
        g_ref[part, 0:NB] = g0
        g_ref[part, NB:] = l1

    unit = jnp.where(iota((NB, NB), 0) == iota((NB, NB), 1), -1.0, 0.0)

    @pl.when(me == 0)
    def _():
        g_ref[0:NB, 0:NB] = unit
        g_ref[0:NB, NB:] = jnp.zeros((NB, NB), jnp.float32)

    @pl.when(me == 1)
    def _():
        g_ref[0:NB, 0:NB] = l0b_full
        g_ref[0:NB, NB:] = unit
        fac_ref[0:NB, :] = l0b_full

    @pl.when(z > 0)
    def _():
        spread(1, 0).wait_recv()
        pass_on(1).start()

    from_sibling(1).wait_recv()
    for j, val in enumerate(factors(side[0], side[1])):
        side_g[0 : DEV * both, j * NB : (j + 1) * NB] = val
    for i in range(4):
        for h, g in enumerate(halves):
            g.far(1, i, items[h][i])

    for kind in range(2):
        pass_on(kind).wait_send()

    @pl.when(is_root)
    def _():
        for kind in range(2):
            for i in range(3):
                spread(kind, i).wait_send()
        for j in range(len(plane)):
            top_send(j).wait_send()

    for half in range(2):

        @pl.when(me == half)
        def _():
            for copy in deal_out(half):
                copy.wait_send()

    for copy in sends:
        copy.wait_send()


def move(k, table, inverses, send, work):
    both = OLD[k]
    dma = pltpu.SemaphoreType.DMA
    outs = ((NT, DEV, NB), (N_OLD[MANY], DEV, NB), (ROWS, 2 * NB), (ROWS, NB), (N_OLD[MANY], 3 * NB))
    scratch = (
        (DEV * k, DEV, NB), (16, DEV, NB), (NB, DEV, NB), (DEV * both, DEV, NB), (NB, DEV, NB),
        (2, ROWS, NB), (2, NT, NB), (2, DEV * both, NB),
    )
    any_ = pl.BlockSpec(memory_space=pl.ANY)
    vmem = pl.BlockSpec(memory_space=pltpu.VMEM)
    return pl.pallas_call(
        functools.partial(move_kernel, k),
        out_shape=tuple(jax.ShapeDtypeStruct(s, jnp.float32) for s in outs),
        in_specs=[pl.BlockSpec(memory_space=pltpu.SMEM), vmem, vmem, any_, any_],
        out_specs=(vmem,) * len(outs),
        scratch_shapes=[pltpu.VMEM(s, jnp.float32) for s in scratch]
        + [
            dma((15,)), dma((15,)), dma((15,)), dma((2,)), dma((15,)), dma((15,)),
            dma((40,)), dma((40,)), dma((PIECES,)), dma((PIECES,)),
            dma((PIECES + 2,)), dma((PIECES + 2,)), dma((15,)), dma((15,)),
            dma((2, 3)), dma((2,)), dma((5,)),
        ],
        compiler_params=pltpu.CompilerParams(
            collective_id=k, has_side_effects=True, vmem_limit_bytes=32 * MIB
        ),
        name=f"move_{k}",
    )(table, table, inverses, send, work)


CHUNKS = 4
CROWS = ROWS // CHUNKS
PITCH = 24


def update_kernel(
    table_ref, place_ref, a_ref, new_ref, old_ref, g_ref, fac_ref, side_ref,
    out_ref,
    a, b3, g3, g, fac, sems,
):
    me = lax.axis_index("prow")
    col = lax.axis_index("pcol")
    few = table_ref[T_OVER, 0] == 0
    parts = [pl.ds(i * CROWS, CROWS) for i in range(CHUNKS)]
    loads = [
        pltpu.make_async_copy(a_ref.at[part], a.at[part, pl.ds(0, DEV)], sems.at[i])
        for i, part in enumerate(parts)
    ]
    for copy in loads:
        copy.start()

    def each_fix(fix):
        @pl.loop(0, table_ref[T_COUNT, 0])
        def _(i):
            entry = table_ref[T_FIX, i]
            src = entry & (NT - 1)
            packed = (src >> 4) * OLD[FEW] + (src & (DEV - 1))
            fix(entry >> 8, jnp.where(few, packed, src))

    g[...] = g_ref[...]
    fac[...] = fac_ref[...]

    def fix_factors(dst, src):
        row = side_ref[pl.ds(src, 1), :]
        g[pl.ds(dst, 1), :] = row[:, NB:]
        fac[pl.ds(dst, 1), :] = row[:, 0:NB]

    each_fix(fix_factors)

    place = place_ref[T_PLACE : T_PLACE + 1, :]
    order_t = jnp.where(iota((NT, NT), 0) == place, 1.0, 0.0).astype(jnp.bfloat16)
    flat = new_ref.reshape(NT * DEV, NB)
    for c in range(DEV):
        hi, lo = split(flat[pl.ds(c, NT, stride=DEV), :])
        for j, val in enumerate((hi, lo, hi)):
            b3[j * NT : (j + 1) * NT, c * NB : (c + 1) * NB] = val
    for part in parts:
        g_hi, g_lo = (
            lax.dot_general(
                val, order_t, (((1,), (1,)), ((), ())), preferred_element_type=jnp.float32
            ).astype(jnp.bfloat16)
            for val in split(g[part, :])
        )
        for j, val in enumerate((g_hi, g_hi, g_lo)):
            g3[part, j * NT : (j + 1) * NT] = val

    aflat = a.reshape(ROWS * PITCH, NB)
    stores = []
    for i, part in enumerate(parts):
        loads[i].wait()

        def fix_row(dst, src):
            @pl.when((dst >> 8) == i)
            def _():
                a[dst, 0:DEV, :] = old_ref[src]

        each_fix(fix_row)
        if i == 0:
            @pl.when(me < 2)
            def _():
                a[0:NB, 0:DEV, :] = jnp.zeros((NB, DEV, NB), jnp.float32)

        for c in range(0, DEV, 2):
            upd = dot(g3[part, :], b3[:, c * NB : (c + 2) * NB])
            for h in range(2):
                where = pl.ds(i * CROWS * PITCH + c + h, CROWS, stride=PITCH)
                val = aflat[where, :] - upd[:, h * NB : (h + 1) * NB]
                if c + h == 0:
                    own = jnp.where(col == 0, fac[part, :], g[part, NB:])
                    if i == 0:
                        keep = jnp.where(col == 0, me == 0, me < 2)
                        own = jnp.where((iota((CROWS, NB), 0) < NB) & keep, val, own)
                    val = jnp.where(col < 2, own, val)
                aflat[where, :] = val
        store = pltpu.make_async_copy(
            a.at[part, pl.ds(0, DEV)], out_ref.at[part], sems.at[CHUNKS + i]
        )
        store.start()
        stores.append(store)
    for store in stores:
        store.wait()


def update(table, work, new, old, g, fac, side):
    any_ = pl.BlockSpec(memory_space=pl.ANY)
    vmem = pl.BlockSpec(memory_space=pltpu.VMEM)
    return pl.pallas_call(
        update_kernel,
        out_shape=jax.ShapeDtypeStruct((ROWS, DEV, NB), jnp.float32),
        in_specs=[pl.BlockSpec(memory_space=pltpu.SMEM), vmem, any_] + [vmem] * 5,
        out_specs=any_,
        scratch_shapes=[
            pltpu.VMEM((ROWS, PITCH, NB), jnp.float32),
            pltpu.VMEM((3 * NT, DEV * NB), jnp.bfloat16),
            pltpu.VMEM((ROWS, 3 * NT), jnp.bfloat16),
            pltpu.VMEM((ROWS, 2 * NB), jnp.float32),
            pltpu.VMEM((ROWS, NB), jnp.float32),
            pltpu.SemaphoreType.DMA((2 * CHUNKS,)),
        ],
        compiler_params=pltpu.CompilerParams(vmem_limit_bytes=40 * MIB),
        name="update",
    )(table, table, work, new, old, g, fac, side)


def on_device(matrix, pivots, block_inverses):
    work = matrix.reshape(ROWS, DEV, NB)
    table, send = plan(FEW, pivots, work)

    def few():
        return move(FEW, table, block_inverses, send, work)

    def many():
        other, rows = plan(MANY, pivots, work)
        return move(MANY, other, block_inverses, rows, work)

    moved = lax.cond(table[T_OVER, 0] == 0, few, many)
    out = update(table, work, *moved)
    return out.reshape(matrix.shape)


def solution(mesh):
    in_specs = (P(None, "prow", None, None, "pcol", None), P(), P())
    out_specs = P(None, "prow", None, None, "pcol", None)
    return jax.shard_map(
        on_device, mesh=mesh, in_specs=in_specs, out_specs=out_specs, check_vma=False
    )
```

```python
import functools

import jax
import jax.numpy as jnp
from jax import lax
from jax.experimental import pallas as pl
from jax.experimental.pallas import tpu as pltpu
from jax.sharding import PartitionSpec as P

MESH = pl.DeviceIdType.MESH
NB = 128
NT = 256
DEV = 16
ROWS = 1024
FEW = 2
MANY = 16
OLD = {FEW: 3, MANY: 16}
N_OLD = {k: DEV * n for k, n in OLD.items()}
MIB = 1 << 20

T_PLACE, T_FIX, T_COUNT, T_PICK, T_OUT, T_MID, T_OVER = range(7)


def iota(shape, dim):
    return lax.broadcasted_iota(jnp.int32, shape, dim)


def fiota(shape, dim):
    return iota(shape, dim).astype(jnp.float32)


def plan_kernel(k, piv_ref, a_ref, table_ref, send_ref, over_ref, row_buf, row_smem, sem, row_sem):
    me = lax.axis_index("prow")
    old = OLD[k]
    sq = (NT, NT)
    sub, lane = fiota(sq, 0), fiota(sq, 1)
    diag = sub == lane
    lane1 = fiota((1, NT), 1)

    def to_col(row):
        row = row.astype(jnp.float32)
        return jnp.sum(jnp.where(diag, row, 0.0), axis=1, keepdims=True)

    def down(mask, value=1.0):
        return jnp.sum(jnp.where(mask, value, 0.0), axis=0, keepdims=True)

    def count(mask):
        return down(mask).astype(jnp.int32)

    def deal(cond, slot, value):
        slot_col = to_col(jnp.where(cond, slot, -1))
        return down(slot_col == lane, to_col(value)).astype(jnp.int32)

    def put(row, value):
        table_ref[row : row + 1, :] = jnp.broadcast_to(value, (1, NT)).astype(jnp.int32)

    piv = piv_ref[...].astype(jnp.float32)
    t_row = jnp.concatenate([piv[0:1, :], piv[1:2, :] + float(NB)], axis=1)
    t_col = to_col(t_row)
    before = sub < lane
    same = t_col == t_row
    last_same = jnp.max(jnp.where(same & before, sub, -1.0), axis=0, keepdims=True)
    later = jnp.max(jnp.where(same & (sub > lane), 1.0, 0.0), axis=0, keepdims=True)
    parent = jnp.max(jnp.where((t_col == lane) & before, sub, -1.0), axis=0, keepdims=True)
    c_row = jnp.where(parent < 0.0, lane1, parent)

    def jump(carry):
        _, c_row = carry
        further = down(sub == c_row, to_col(c_row))
        return jnp.max(jnp.abs(further - c_row)) > 0.5, further

    _, c_row = lax.while_loop(lambda carry: carry[0], jump, (jnp.bool_(True), c_row))

    from_swap = down(sub == last_same, to_col(c_row))
    src = jnp.where(last_same < 0.0, t_row, from_swap).astype(jnp.int32)
    owner = (src >> 7) & (DEV - 1)
    local = ((src >> 11) << 7) + (src & (NB - 1))
    owner_row, owner_col = owner.astype(jnp.float32), to_col(owner)
    less = owner_col < owner_row
    pos = count(less | ((owner_col == owner_row) & before))
    rank = pos - count(less)
    bin_, which = pos & (DEV - 1), rank >> 4
    send = deal((owner == me) & (which < k), bin_ * k + which, local)
    row_buf[0:1, :] = send
    to_smem = pltpu.make_async_copy(row_buf, row_smem, sem)
    to_smem.start()

    put(T_PLACE, bin_ * 16 + (pos >> 4))
    put(T_PICK, deal(bin_ == me, pos >> 4, owner * k + jnp.minimum(which, k - 1)))

    target, c = t_row.astype(jnp.int32), c_row.astype(jnp.int32)
    goes = (later < 0.5) & (target >= NT)
    to, block = (target >> 7) & (DEV - 1), c >> 7
    key = jnp.where(goes, block * DEV + to, 64)
    key_row, key_col = key.astype(jnp.float32), to_col(key)
    less = key_col < key_row
    pos = count(less | ((key_col == key_row) & before))
    pos = pos - count(key_col < (block * DEV).astype(jnp.float32))
    mid, slot = pos & (DEV - 1), pos >> 4
    pair = jnp.where(goes, to * DEV + mid, NT)
    turn = count((to_col(pair) == pair.astype(jnp.float32)) & before)
    put(T_OUT, deal(goes & (block == me), mid * 8 + slot, c & (NB - 1)))
    put(T_MID, deal(goes & (turn < old) & (mid == me), to * old + turn, block * 8 + slot))
    mine = goes & (to == me)
    order = count(before & (to_col(jnp.where(mine, 1, 0)) > 0.5))
    dst = ((target >> 11) << 7) + (target & (NB - 1))
    put(T_FIX, deal(mine, order, dst * NT + mid * DEV + turn))
    put(T_COUNT, jnp.sum(jnp.where(mine, 1.0, 0.0), axis=1, keepdims=True))
    over = (which >= k) | (goes & (turn >= old))
    any_over = jnp.max(jnp.where(over, 1.0, 0.0), axis=1, keepdims=True)
    put(T_OVER, any_over)
    over_ref[0, 0] = (jnp.max(any_over) > 0.5).astype(jnp.int32)
    put(7, jnp.zeros((1, 1), jnp.int32))

    to_smem.wait()
    copies = [
        pltpu.make_async_copy(a_ref.at[row_smem[0, i]], send_ref.at[i], row_sem.at[i])
        for i in range(DEV * k)
    ]
    for copy in copies:
        copy.start()
    for copy in copies:
        copy.wait()


def plan(k, pivots, work):
    return pl.pallas_call(
        functools.partial(plan_kernel, k),
        out_shape=(
            jax.ShapeDtypeStruct((8, NT), jnp.int32),
            jax.ShapeDtypeStruct((DEV * k, DEV, NB), jnp.float32),
            jax.ShapeDtypeStruct((1, 1), jnp.int32),
        ),
        in_specs=[pl.BlockSpec(memory_space=pltpu.VMEM), pl.BlockSpec(memory_space=pl.ANY)],
        out_specs=(
            pl.BlockSpec(memory_space=pltpu.VMEM),
            pl.BlockSpec(memory_space=pl.ANY),
            pl.BlockSpec(memory_space=pltpu.SMEM),
        ),
        scratch_shapes=[
            pltpu.VMEM((8, NT), jnp.int32),
            pltpu.SMEM((8, NT), jnp.int32),
            pltpu.SemaphoreType.DMA,
            pltpu.SemaphoreType.DMA((DEV * k,)),
        ],
        name=f"plan_{k}",
    )(pivots, work)


def split(a):
    hi = a.astype(jnp.bfloat16)
    return hi, (a - hi.astype(jnp.float32)).astype(jnp.bfloat16)


def dot(a, b):
    return jnp.dot(a, b, preferred_element_type=jnp.float32)


def dot3(a, b):
    return dot(a[0], b[0]) + (dot(a[0], b[1]) + dot(a[1], b[0]))


X_FIRST = 10
PIECES = 2


def move_kernel(
    k, table_ref, place_ref, inv_ref, send_ref, a_ref,
    b_hi, b_lo, g_hi, g_lo, fac_ref, old_out, side_out,
    got, mid, leave, leave2, first, new, panel, top, side, old, side_g,
    s_got, r_got, s_out, r_out, s_mid, r_mid, s_ag, r_ag, s_z, r_z, s_sib, r_sib,
    s_top, r_top, s_far, r_far, s_loc,
):
    me = lax.axis_index("prow")
    col = lax.axis_index("pcol")
    x, y = me // 4, me % 4
    z, core = col // 2, col % 2
    both = OLD[k]
    sends = []
    is_root, is_old = z == 0, me < 2

    def at(px, py):
        return (lax.rem(px + 4, 4) * 4 + lax.rem(py + 4, 4), col)

    def remote(src, dst, send_sem, recv_sem, device):
        return pltpu.make_async_remote_copy(
            src_ref=src, dst_ref=dst, send_sem=send_sem, recv_sem=recv_sem,
            device_id=device, device_id_type=MESH,
        )

    offsets = [(dx, dy) for dx in range(4) for dy in range(4) if (dx, dy) != (0, 0)]
    plane = [at(x + dx, y + dy) for dx, dy in offsets]
    origin = [at(x - dx, y - dy) for dx, dy in offsets]
    sibling = (me, z * 2 + 1 - core)
    others = [(me, lax.rem(z + i, 4) * 2 + core) for i in (1, 2, 3)]

    mine = pltpu.make_async_copy(a_ref.at[:, 0, :], panel.at[core], s_loc.at[0])
    block = pltpu.make_async_copy(a_ref.at[pl.ds(0, NB)], first, s_loc.at[1])

    @pl.when(is_root)
    def _():
        mine.start()

    @pl.when(is_old)
    def _():
        block.start()

    barrier = pltpu.get_barrier_semaphore()
    greeted = plane + others + [sibling]
    for device in greeted:
        pl.semaphore_signal(barrier, inc=1, device_id=device, device_id_type=MESH)

    @pl.when(is_old)
    def _():
        block.wait()

        @pl.loop(0, NB)
        def _(i):
            leave[i] = first[table_ref[T_OUT, i]]

    pl.semaphore_wait(barrier, len(greeted))

    def exchange(src, dst, n, s_sem, r_sem):
        for j, device in enumerate(plane):
            copy = remote(
                src.at[pl.ds(device[0] * n, n)], dst.at[pl.ds(me * n, n)],
                s_sem.at[j], r_sem.at[j], device,
            )
            copy.start()
            sends.append(copy)

    def exchanged(src, dst, n, s_sem, r_sem):
        for j, device in enumerate(origin):
            remote(
                src.at[pl.ds(0, n)], dst.at[pl.ds(device[0] * n, n)],
                s_sem.at[j], r_sem.at[j], device,
            ).wait_recv()

    exchange(send_ref, got, k, s_got, r_got)
    own = pltpu.make_async_copy(
        send_ref.at[pl.ds(me * k, k)], got.at[pl.ds(me * k, k)], s_loc.at[2]
    )
    own.start()

    size = ROWS // PIECES

    def z_part(which, i):
        return panel.at[which, pl.ds(i * size, size)]

    def z_out(i, j):
        ref = z_part(core, i)
        return remote(ref, ref, s_z.at[i, j], r_z.at[i], others[j])

    def z_sibling(which, i):
        ref = z_part(which, i)
        return remote(ref, ref, s_sib.at[i], r_sib.at[i], sibling)

    def z_step(i):
        @pl.when(z > 0)
        def _():
            z_out(i, 0).wait_recv()
            z_sibling(core, i).start()

    def z_finish(i):
        z_sibling(core, i).wait_send()
        z_sibling(1 - core, i).wait_recv()

    @pl.when(is_root)
    def _():
        mine.wait()
        for i in range(PIECES):
            for j in range(3):
                z_out(i, j).start()
            z_sibling(core, i).start()

    def deal_out(half):
        return [
            remote(
                leave.at[pl.ds(device[0] * 8, 8)], mid.at[pl.ds(half * 8, 8)],
                s_out.at[j], r_out.at[half], device,
            )
            for j, device in enumerate(plane)
        ]

    def deal_own(half):
        return pltpu.make_async_copy(
            leave.at[pl.ds(me * 8, 8)], mid.at[pl.ds(half * 8, 8)], s_loc.at[3]
        )

    for half in range(2):

        @pl.when(me == half)
        def _():
            deal_own(half).start()
            for copy in deal_out(half):
                copy.start()

    def ring(axis, step):
        if axis == 0:
            return lax.rem(x + step + 4, 4) * 4 + y
        return x * 4 + lax.rem(y + step + 4, 4)

    def shifted(index, axis, step):
        px, py = index // 4, index % 4
        if axis == 0:
            return lax.rem(px + step + 4, 4) * 4 + py
        return px * 4 + lax.rem(py + step + 4, 4)

    def part_of(index, half, part=None):
        first_row, n = (0, X_FIRST) if half == 0 else (X_FIRST, 16 - X_FIRST)
        if part is not None:
            n = n // 2
            first_row += part * n
        return new.at[pl.ds(index * 16 + first_row, n)]

    class Gather:
        def __init__(self, half):
            self.half, self.base = half, half * 20
            self.axes = (0, 1) if half == 0 else (1, 0)

        def copy(self, phase, item, role, index, part=None, step=None):
            n = self.base + phase * (1 + item) * 4 + role
            ref = part_of(index, self.half, part)
            if step is None:
                step = 1 if role % 2 == 0 else 3
            return remote(ref, ref, s_ag.at[n], r_ag.at[n], (ring(self.axes[phase], step), col))

        def send(self, *args, **kw):
            copy = self.copy(*args, **kw)
            copy.start()
            sends.append(copy)

        def start(self, phase, item, index):
            for role in range(2):
                self.send(phase, item, role, index)
            if phase == 0:
                self.send(phase, item, 2, index, step=2)

        def near(self, phase, item, index, role):
            came = shifted(index, self.axes[phase], 3 if role == 0 else 1)
            self.copy(phase, item, role, came).wait_recv()
            if phase == 1:
                self.send(phase, item, 2 + role, came, role)
            return came

        def far(self, phase, item, index):
            came = shifted(index, self.axes[phase], 2)
            if phase == 0:
                self.copy(phase, item, 2, came, step=2).wait_recv()
                return came
            for role in range(2):
                self.copy(phase, item, 2 + role, came, role).wait_recv()
            return came

    exchanged(send_ref, got, k, s_got, r_got)
    own.wait()
    for i in range(16):
        new[me * 16 + i] = got[table_ref[T_PICK, i]]
    flat = new.reshape(NT * DEV, NB)

    def convert(dx, dy):
        index = at(x + dx, y + dy)[0]
        rows = pl.ds(pl.multiple_of(index * 16, 16), 16)
        for c in range(DEV):
            hi, lo = split(flat[pl.ds(index * 16 * DEV + c, 16, stride=DEV), :])
            b_hi[rows, c * NB : (c + 1) * NB] = hi
            b_lo[rows, c * NB : (c + 1) * NB] = lo

    halves = [Gather(h) for h in range(2)]
    items = [[me], [me]]
    for g in halves:
        g.start(0, 0, me)
    for g in halves:
        g.start(1, 0, me)

    def top_part(index):
        return top.at[core, pl.ds(index * 16, 16)]

    def top_send(j):
        return remote(top_part(me), top_part(me), s_top.at[j], r_top.at[j], plane[j])

    def spread(kind, i):
        ref = (top if kind == 0 else side).at[core]
        return remote(ref, ref, s_far.at[kind, i], r_far.at[kind], others[i])

    def pass_on(kind):
        ref = (top if kind == 0 else side).at[core]
        n = PIECES + kind
        return remote(ref, ref, s_sib.at[n], r_sib.at[n], sibling)

    def from_sibling(kind):
        ref = (top if kind == 0 else side).at[1 - core]
        n = PIECES + kind
        return remote(ref, ref, s_sib.at[n], r_sib.at[n], sibling)

    @pl.when(is_root)
    def _():
        top[core, pl.ds(me * 16, 16), :] = new.reshape(NT * DEV, NB)[
            pl.ds(me * 16 * DEV, 16, stride=DEV), :
        ]
        for j in range(len(plane)):
            top_send(j).start()

    convert(0, 0)
    for role in range(2):
        for h, g in enumerate(halves):
            came = g.near(0, 0, me, role)
            g.start(1, 1 + role, came)
            items[h].append(came)
    for h, g in enumerate(halves):
        came = g.far(0, 0, me)
        g.start(1, 3, came)
        items[h].append(came)

    for half in range(2):

        @pl.when(me == half)
        def _():
            deal_own(half).wait()

        @pl.when(me != half)
        def _():
            ref = mid.at[pl.ds(half * 8, 8)]
            remote(ref, ref, s_out.at[0], r_out.at[half], plane[0]).wait_recv()

    for i in range(DEV * both):
        leave2[i] = mid[table_ref[T_MID, i]]
    exchange(leave2, old, both, s_mid, r_mid)
    own_old = pltpu.make_async_copy(
        leave2.at[pl.ds(me * both, both)], old.at[pl.ds(me * both, both)], s_loc.at[4]
    )
    own_old.start()


    @pl.when(is_root)
    def _():
        for j in range(len(plane)):
            index = origin[j][0]
            remote(
                top_part(index), top_part(index), s_top.at[j], r_top.at[j], plane[j]
            ).wait_recv()
        for i in range(3):
            spread(0, i).start()
        pass_on(0).start()

    def forward(i):
        for h, g in enumerate(halves):
            for role in range(2):
                g.near(1, i, items[h][i], role)


    forward(0)
    forward(1)

    @pl.when(z > 0)
    def _():
        spread(0, 0).wait_recv()
        pass_on(0).start()

    forward(2)
    forward(3)
    for i in range(PIECES):
        z_step(i)
    exchanged(leave2, old, both, s_mid, r_mid)
    own_old.wait()
    outs = [
        pltpu.make_async_copy(old, old_out.at[pl.ds(0, DEV * both)], s_loc.at[5]),
        pltpu.make_async_copy(side_g, side_out.at[pl.ds(0, DEV * both)], s_loc.at[6]),
    ]
    outs[0].start()

    @pl.when(is_root)
    def _():
        side[core] = old.reshape(DEV * both * DEV, NB)[pl.ds(0, DEV * both, stride=DEV), :]
        for i in range(3):
            spread(1, i).start()
        pass_on(1).start()

    for i in range(PIECES):
        z_finish(i)
    from_sibling(0).wait_recv()

    place = place_ref[T_PLACE : T_PLACE + 1, :]
    order_t = jnp.where(iota((NT, NT), 0) == place, 1.0, 0.0).astype(jnp.bfloat16)

    def pick(lo, val):
        return lax.dot_general(
            order_t[:, lo : lo + NB], val, (((0,), (0,)), ((), ())),
            preferred_element_type=jnp.float32,
        ).astype(jnp.bfloat16)

    inv = [split(inv_ref[s]) for s in range(2)]
    u0p = tuple(pick(0, v) for v in split(top[1]))
    l0b_full = dot3(tuple(pick(NB, v) for v in split(top[0])), inv[0])
    l0b = split(l0b_full)

    def factors(p0, p1):
        l0 = dot3(split(p0), inv[0])
        l1 = dot3(split(p1 - dot3(split(l0), u0p)), inv[1])
        return l0, l0 - dot3(split(l1), l0b), l1

    def placed(g0, l1):
        return [
            lax.dot_general(
                val, order_t, (((1,), (1,)), ((), ())), preferred_element_type=jnp.float32
            )
            for val in split(jnp.concatenate([g0, l1], axis=1))
        ]

    def keep_factors(part, l0, g0, l1):
        fac_ref[part, :] = jnp.where(col == 0, l0, l1)
        for ref, val in zip((g_hi, g_lo), placed(g0, l1)):
            ref[part, :] = val.astype(jnp.bfloat16)

    for i in range(4):
        part = pl.ds(i * 256, 256)
        keep_factors(part, *factors(panel[0, part, :], panel[1, part, :]))

    unit = jnp.where(iota((NB, NB), 0) == iota((NB, NB), 1), -1.0, 0.0)
    none = jnp.zeros((NB, NB), jnp.float32)

    @pl.when(me == 0)
    def _():
        keep_factors(pl.ds(0, NB), none, unit, none)

    @pl.when(me == 1)
    def _():
        keep_factors(pl.ds(0, NB), l0b_full, l0b_full, unit)

    @pl.when(z > 0)
    def _():
        spread(1, 0).wait_recv()
        pass_on(1).start()

    from_sibling(1).wait_recv()
    l0, g0, l1 = factors(side[0], side[1])
    for val, lanes in zip(placed(g0, l1), (slice(0, NT), slice(NT, 2 * NT))):
        side_g[:, lanes] = val
    side_g[:, 2 * NT :] = jnp.where(col == 0, l0, l1)
    outs[1].start()
    for dx, dy in offsets:
        if dx != 2 and dy != 2:
            convert(dx, dy)
    for i in range(4):
        for h, g in enumerate(halves):
            g.far(1, i, items[h][i])
    for dx, dy in offsets:
        if dx == 2 or dy == 2:
            convert(dx, dy)

    for kind in range(2):
        pass_on(kind).wait_send()

    @pl.when(is_root)
    def _():
        for kind in range(2):
            for i in range(3):
                spread(kind, i).wait_send()
        for i in range(PIECES):
            for j in range(3):
                z_out(i, j).wait_send()
        for j in range(len(plane)):
            top_send(j).wait_send()

    for half in range(2):

        @pl.when(me == half)
        def _():
            for copy in deal_out(half):
                copy.wait_send()

    for copy in sends:
        copy.wait_send()
    for copy in outs:
        copy.wait()


def move(k, table, inverses, send, work):
    both = OLD[k]
    dma = pltpu.SemaphoreType.DMA
    f32, b16 = jnp.float32, jnp.bfloat16
    outs = (
        ((NT, DEV * NB), b16), ((NT, DEV * NB), b16),
        ((ROWS, NT), b16), ((ROWS, NT), b16), ((ROWS, NB), f32),
        ((N_OLD[MANY], DEV, NB), f32), ((N_OLD[MANY], 2 * NT + NB), f32),
    )
    scratch = (
        (DEV * k, DEV, NB), (16, DEV, NB), (NB, DEV, NB), (DEV * both, DEV, NB), (NB, DEV, NB),
        (NT, DEV, NB), (2, ROWS, NB), (2, NT, NB), (2, DEV * both, NB), (DEV * both, DEV, NB),
        (DEV * both, 2 * NT + NB),
    )
    any_ = pl.BlockSpec(memory_space=pl.ANY)
    vmem = pl.BlockSpec(memory_space=pltpu.VMEM)
    return pl.pallas_call(
        functools.partial(move_kernel, k),
        out_shape=tuple(jax.ShapeDtypeStruct(*s) for s in outs),
        in_specs=[pl.BlockSpec(memory_space=pltpu.SMEM), vmem, vmem, any_, any_],
        out_specs=(vmem,) * 5 + (pl.BlockSpec(memory_space=pltpu.HBM),) * 2,
        scratch_shapes=[pltpu.VMEM(s, jnp.float32) for s in scratch]
        + [
            dma((15,)), dma((15,)), dma((15,)), dma((2,)), dma((15,)), dma((15,)),
            dma((40,)), dma((40,)), dma((PIECES, 3)), dma((PIECES,)),
            dma((PIECES + 2,)), dma((PIECES + 2,)), dma((15,)), dma((15,)),
            dma((2, 3)), dma((2,)), dma((7,)),
        ],
        compiler_params=pltpu.CompilerParams(
            collective_id=k, has_side_effects=True, vmem_limit_bytes=(14 if k == FEW else 20) * MIB
        ),
        name=f"move_{k}",
    )(table, table, inverses, send, work)


CHUNKS = 4
CROWS = ROWS // CHUNKS
PITCH = 24


def update_kernel(
    table_ref, a_ref, b_hi, b_lo, hi_ref, lo_ref, fac_ref, old_ref, side_ref,
    out_ref,
    a, g_hi, g_lo, fac, old, side, sems, old_sems,
):
    me = lax.axis_index("prow")
    col = lax.axis_index("pcol")
    few = table_ref[T_OVER, 0] == 0
    parts = [pl.ds(i * CROWS, CROWS) for i in range(CHUNKS)]

    def old_loads(n):
        part = pl.ds(0, n)
        return [
            pltpu.make_async_copy(old_ref.at[part], old.at[part], old_sems.at[0]),
            pltpu.make_async_copy(side_ref.at[part], side.at[part], old_sems.at[1]),
        ]

    def each_old(do):
        for cond, k in ((few, FEW), (jnp.logical_not(few), MANY)):

            @pl.when(cond)
            def _():
                for copy in old_loads(N_OLD[k]):
                    do(copy)

    each_old(lambda copy: copy.start())
    loads = [
        pltpu.make_async_copy(a_ref.at[part], a.at[part, pl.ds(0, DEV)], sems.at[i])
        for i, part in enumerate(parts)
    ]
    for copy in loads[:2]:
        copy.start()

    def each_fix(fix):
        @pl.loop(0, table_ref[T_COUNT, 0])
        def _(i):
            entry = table_ref[T_FIX, i]
            src = entry & (NT - 1)
            packed = (src >> 4) * OLD[FEW] + (src & (DEV - 1))
            fix(entry >> 8, jnp.where(few, packed, src))

    aflat = a.reshape(ROWS * PITCH, NB)
    g_hi[...] = hi_ref[...].astype(jnp.float32)
    g_lo[...] = lo_ref[...].astype(jnp.float32)
    fac[...] = fac_ref[...]

    def fix_factors(dst, src):
        row = side[pl.ds(src, 1), :]
        g_hi[pl.ds(dst, 1), :] = row[:, :NT]
        g_lo[pl.ds(dst, 1), :] = row[:, NT : 2 * NT]
        fac[pl.ds(dst, 1), :] = row[:, 2 * NT :]

    each_old(lambda copy: copy.wait())
    each_fix(fix_factors)
    stores = []
    for i, part in enumerate(parts):
        hi, lo = g_hi[part, :].astype(jnp.bfloat16), g_lo[part, :].astype(jnp.bfloat16)
        left = jnp.concatenate([hi, hi, lo], axis=1)
        loads[i].wait()
        if i + 2 < CHUNKS:
            loads[i + 2].start()

        def fix_row(dst, src):
            @pl.when(dst // CROWS == i)
            def _():
                a[dst, 0:DEV, :] = old[src]

        each_fix(fix_row)
        if i == 0:
            @pl.when(me < 2)
            def _():
                a[0:NB, 0:DEV, :] = jnp.zeros((NB, DEV, NB), jnp.float32)

        for c in range(0, DEV, 2):
            wide = slice(c * NB, (c + 2) * NB)
            right = jnp.concatenate([b_hi[:, wide], b_lo[:, wide], b_hi[:, wide]], axis=0)
            upd = dot(left, right)
            for h in range(2):
                where = pl.ds(i * CROWS * PITCH + c + h, CROWS, stride=PITCH)
                val = aflat[where, :] - upd[:, h * NB : (h + 1) * NB]
                if c + h == 0:
                    own = fac[part, :]
                    if i == 0:
                        keep = jnp.where(col == 0, me == 0, me < 2)
                        own = jnp.where((iota((CROWS, NB), 0) < NB) & keep, val, own)
                    val = jnp.where(col < 2, own, val)
                aflat[where, :] = val
        store = pltpu.make_async_copy(
            a.at[part, pl.ds(0, DEV)], out_ref.at[part], sems.at[CHUNKS + i]
        )
        store.start()
        stores.append(store)
    for store in stores:
        store.wait()


def update(table, work, *moved):
    any_ = pl.BlockSpec(memory_space=pl.ANY)
    vmem = pl.BlockSpec(memory_space=pltpu.VMEM)
    return pl.pallas_call(
        update_kernel,
        out_shape=jax.ShapeDtypeStruct((ROWS, DEV, NB), jnp.float32),
        in_specs=[pl.BlockSpec(memory_space=pltpu.SMEM), any_] + [vmem] * 5 + [pl.BlockSpec(memory_space=pltpu.HBM)] * 2,
        out_specs=any_,
        scratch_shapes=[
            pltpu.VMEM((ROWS, PITCH, NB), jnp.float32),
            pltpu.VMEM((ROWS, NT), jnp.float32),
            pltpu.VMEM((ROWS, NT), jnp.float32),
            pltpu.VMEM((ROWS, NB), jnp.float32),
            pltpu.VMEM((N_OLD[MANY], DEV, NB), jnp.float32),
            pltpu.VMEM((N_OLD[MANY], 2 * NT + NB), jnp.float32),
            pltpu.SemaphoreType.DMA((2 * CHUNKS,)),
            pltpu.SemaphoreType.DMA((2,)),
        ],
        compiler_params=pltpu.CompilerParams(vmem_limit_bytes=24 * MIB),
        name="update",
    )(table, work, *moved)


def on_device(matrix, pivots, block_inverses):
    work = matrix.reshape(ROWS, DEV, NB)
    table, send, over = plan(FEW, pivots, work)

    def few():
        return move(FEW, table, block_inverses, send, work)

    def many():
        other, rows, _ = plan(MANY, pivots, work)
        return move(MANY, other, block_inverses, rows, work)

    moved = lax.cond(over.reshape(()) == 0, few, many)
    out = update(table, work, *moved)
    return out.reshape(matrix.shape)


def solution(mesh):
    in_specs = (P(None, "prow", None, None, "pcol", None), P(), P())
    out_specs = P(None, "prow", None, None, "pcol", None)
    return jax.shard_map(
        on_device, mesh=mesh, in_specs=in_specs, out_specs=out_specs, check_vma=False
    )
```

```python
import functools

import jax
import jax.numpy as jnp
from jax import lax
from jax.experimental import pallas as pl
from jax.experimental.pallas import tpu as pltpu
from jax.sharding import PartitionSpec as P

MESH = pl.DeviceIdType.MESH
NB = 128
NT = 256
DEV = 16
ROWS = 1024
FEW = 2
MANY = 16
OLD = {FEW: 3, MANY: 16}
N_OLD = {k: DEV * n for k, n in OLD.items()}
MIB = 1 << 20

T_PLACE, T_FIX, T_COUNT, T_PICK, T_OUT, T_MID, T_OVER = range(7)


def iota(shape, dim):
    return lax.broadcasted_iota(jnp.int32, shape, dim)


def fiota(shape, dim):
    return iota(shape, dim).astype(jnp.float32)


def plan_kernel(k, piv_ref, a_ref, table_ref, send_ref, over_ref, row_buf, row_smem, sem, row_sem):
    me = lax.axis_index("prow")
    old = OLD[k]
    sq = (NT, NT)
    sub, lane = fiota(sq, 0), fiota(sq, 1)
    diag = sub == lane
    lane1 = fiota((1, NT), 1)

    def to_col(row):
        row = row.astype(jnp.float32)
        return jnp.sum(jnp.where(diag, row, 0.0), axis=1, keepdims=True)

    def down(mask, value=1.0):
        return jnp.sum(jnp.where(mask, value, 0.0), axis=0, keepdims=True)

    def count(mask):
        return down(mask).astype(jnp.int32)

    def deal(cond, slot, value):
        slot_col = to_col(jnp.where(cond, slot, -1))
        return down(slot_col == lane, to_col(value)).astype(jnp.int32)

    def put(row, value):
        table_ref[row : row + 1, :] = jnp.broadcast_to(value, (1, NT)).astype(jnp.int32)

    piv = piv_ref[...].astype(jnp.float32)
    t_row = jnp.concatenate([piv[0:1, :], piv[1:2, :] + float(NB)], axis=1)
    t_col = to_col(t_row)
    before = sub < lane
    same = t_col == t_row
    last_same = jnp.max(jnp.where(same & before, sub, -1.0), axis=0, keepdims=True)
    later = jnp.max(jnp.where(same & (sub > lane), 1.0, 0.0), axis=0, keepdims=True)
    parent = jnp.max(jnp.where((t_col == lane) & before, sub, -1.0), axis=0, keepdims=True)
    c_row = jnp.where(parent < 0.0, lane1, parent)

    def jump(carry):
        _, c_row = carry
        further = down(sub == c_row, to_col(c_row))
        return jnp.max(jnp.abs(further - c_row)) > 0.5, further

    _, c_row = lax.while_loop(lambda carry: carry[0], jump, (jnp.bool_(True), c_row))

    from_swap = down(sub == last_same, to_col(c_row))
    src = jnp.where(last_same < 0.0, t_row, from_swap).astype(jnp.int32)
    owner = (src >> 7) & (DEV - 1)
    local = ((src >> 11) << 7) + (src & (NB - 1))
    owner_row, owner_col = owner.astype(jnp.float32), to_col(owner)
    less = owner_col < owner_row
    pos = count(less | ((owner_col == owner_row) & before))
    rank = pos - count(less)
    bin_, which = pos & (DEV - 1), rank >> 4
    send = deal((owner == me) & (which < k), bin_ * k + which, local)
    row_buf[0:1, :] = send
    to_smem = pltpu.make_async_copy(row_buf, row_smem, sem)
    to_smem.start()

    put(T_PLACE, bin_ * 16 + (pos >> 4))
    put(T_PICK, deal(bin_ == me, pos >> 4, owner * k + jnp.minimum(which, k - 1)))

    target, c = t_row.astype(jnp.int32), c_row.astype(jnp.int32)
    goes = (later < 0.5) & (target >= NT)
    to, block = (target >> 7) & (DEV - 1), c >> 7
    key = jnp.where(goes, block * DEV + to, 64)
    key_row, key_col = key.astype(jnp.float32), to_col(key)
    less = key_col < key_row
    pos = count(less | ((key_col == key_row) & before))
    pos = pos - count(key_col < (block * DEV).astype(jnp.float32))
    mid, slot = pos & (DEV - 1), pos >> 4
    pair = jnp.where(goes, to * DEV + mid, NT)
    turn = count((to_col(pair) == pair.astype(jnp.float32)) & before)
    put(T_OUT, deal(goes & (block == me), mid * 8 + slot, c & (NB - 1)))
    put(T_MID, deal(goes & (turn < old) & (mid == me), to * old + turn, block * 8 + slot))
    mine = goes & (to == me)
    order = count(before & (to_col(jnp.where(mine, 1, 0)) > 0.5))
    dst = ((target >> 11) << 7) + (target & (NB - 1))
    put(T_FIX, deal(mine, order, dst * NT + mid * DEV + turn))
    put(T_COUNT, jnp.sum(jnp.where(mine, 1.0, 0.0), axis=1, keepdims=True))
    over = (which >= k) | (goes & (turn >= old))
    any_over = jnp.max(jnp.where(over, 1.0, 0.0), axis=1, keepdims=True)
    put(T_OVER, any_over)
    over_ref[0, 0] = (jnp.max(any_over) > 0.5).astype(jnp.int32)
    put(7, jnp.zeros((1, 1), jnp.int32))

    to_smem.wait()
    copies = [
        pltpu.make_async_copy(a_ref.at[row_smem[0, i]], send_ref.at[i], row_sem.at[i])
        for i in range(DEV * k)
    ]
    for copy in copies:
        copy.start()
    for copy in copies:
        copy.wait()


def plan(k, pivots, work):
    return pl.pallas_call(
        functools.partial(plan_kernel, k),
        out_shape=(
            jax.ShapeDtypeStruct((8, NT), jnp.int32),
            jax.ShapeDtypeStruct((DEV * k, DEV, NB), jnp.float32),
            jax.ShapeDtypeStruct((1, 1), jnp.int32),
        ),
        in_specs=[pl.BlockSpec(memory_space=pltpu.VMEM), pl.BlockSpec(memory_space=pl.ANY)],
        out_specs=(
            pl.BlockSpec(memory_space=pltpu.VMEM),
            pl.BlockSpec(memory_space=pl.ANY),
            pl.BlockSpec(memory_space=pltpu.SMEM),
        ),
        scratch_shapes=[
            pltpu.VMEM((8, NT), jnp.int32),
            pltpu.SMEM((8, NT), jnp.int32),
            pltpu.SemaphoreType.DMA,
            pltpu.SemaphoreType.DMA((DEV * k,)),
        ],
        name=f"plan_{k}",
    )(pivots, work)


def split(a):
    hi = a.astype(jnp.bfloat16)
    return hi, (a - hi.astype(jnp.float32)).astype(jnp.bfloat16)


def dot(a, b):
    return jnp.dot(a, b, preferred_element_type=jnp.float32)


def dot3(a, b):
    return dot(a[0], b[0]) + (dot(a[0], b[1]) + dot(a[1], b[0]))


X_FIRST = 10
PIECES = 2


def move_kernel(
    k, table_ref, place_ref, inv_ref, send_ref, a_ref,
    b_hi, b_lo, g_hi, g_lo, fac_ref, old_out, side_out,
    got, mid, leave, leave2, first, wide, new, panel, top, side, old, side_g,
    s_got, r_got, s_out, r_out, s_mid, r_mid, s_ag, r_ag, s_z, r_z, s_sib, r_sib,
    s_top, r_top, s_far, r_far, s_loc,
):
    me = lax.axis_index("prow")
    col = lax.axis_index("pcol")
    x, y = me // 4, me % 4
    z, core = col // 2, col % 2
    both = OLD[k]
    sends = []
    is_root, is_old = z == 0, me < 2

    def at(px, py):
        return (lax.rem(px + 4, 4) * 4 + lax.rem(py + 4, 4), col)

    def remote(src, dst, send_sem, recv_sem, device):
        return pltpu.make_async_remote_copy(
            src_ref=src, dst_ref=dst, send_sem=send_sem, recv_sem=recv_sem,
            device_id=device, device_id_type=MESH,
        )

    offsets = [(dx, dy) for dx in range(4) for dy in range(4) if (dx, dy) != (0, 0)]
    plane = [at(x + dx, y + dy) for dx, dy in offsets]
    origin = [at(x - dx, y - dy) for dx, dy in offsets]
    sibling = (me, z * 2 + 1 - core)
    others = [(me, lax.rem(z + i, 4) * 2 + core) for i in (1, 2, 3)]

    mine = pltpu.make_async_copy(a_ref.at[:, pl.ds(0, 8)], wide, s_loc.at[0])
    block = pltpu.make_async_copy(a_ref.at[pl.ds(0, NB)], first, s_loc.at[1])

    @pl.when(is_root)
    def _():
        mine.start()

    @pl.when(is_old)
    def _():
        block.start()

    barrier = pltpu.get_barrier_semaphore()
    greeted = plane + others + [sibling]
    for device in greeted:
        pl.semaphore_signal(barrier, inc=1, device_id=device, device_id_type=MESH)

    @pl.when(is_old)
    def _():
        block.wait()

        @pl.loop(0, NB)
        def _(i):
            leave[i] = first[table_ref[T_OUT, i]]

    pl.semaphore_wait(barrier, len(greeted))

    def exchange(src, dst, n, s_sem, r_sem):
        for j, device in enumerate(plane):
            copy = remote(
                src.at[pl.ds(device[0] * n, n)], dst.at[pl.ds(me * n, n)],
                s_sem.at[j], r_sem.at[j], device,
            )
            copy.start()
            sends.append(copy)

    def exchanged(src, dst, n, s_sem, r_sem):
        for j, device in enumerate(origin):
            remote(
                src.at[pl.ds(0, n)], dst.at[pl.ds(device[0] * n, n)],
                s_sem.at[j], r_sem.at[j], device,
            ).wait_recv()

    size = ROWS // PIECES

    def z_part(which, i):
        return panel.at[which, pl.ds(i * size, size)]

    def z_out(i, j):
        ref = z_part(core, i)
        return remote(ref, ref, s_z.at[i, j], r_z.at[i], others[j])

    def z_sibling(which, i):
        ref = z_part(which, i)
        return remote(ref, ref, s_sib.at[i], r_sib.at[i], sibling)

    def z_step(i):
        @pl.when(z > 0)
        def _():
            z_out(i, 0).wait_recv()
            z_sibling(core, i).start()

    def z_finish(i):
        z_sibling(core, i).wait_send()
        z_sibling(1 - core, i).wait_recv()

    @pl.when(is_root)
    def _():
        mine.wait()
        panel[core] = wide.reshape(ROWS * 8, NB)[pl.ds(0, ROWS, stride=8), :]
        for i in range(PIECES):
            for j in range(3):
                z_out(i, j).start()
            z_sibling(core, i).start()

    exchange(send_ref, got, k, s_got, r_got)
    own = pltpu.make_async_copy(
        send_ref.at[pl.ds(me * k, k)], got.at[pl.ds(me * k, k)], s_loc.at[2]
    )
    own.start()

    def deal_out(half):
        return [
            remote(
                leave.at[pl.ds(device[0] * 8, 8)], mid.at[pl.ds(half * 8, 8)],
                s_out.at[j], r_out.at[half], device,
            )
            for j, device in enumerate(plane)
        ]

    def deal_own(half):
        return pltpu.make_async_copy(
            leave.at[pl.ds(me * 8, 8)], mid.at[pl.ds(half * 8, 8)], s_loc.at[3]
        )

    for half in range(2):

        @pl.when(me == half)
        def _():
            deal_own(half).start()
            for copy in deal_out(half):
                copy.start()

    def ring(axis, step):
        if axis == 0:
            return lax.rem(x + step + 4, 4) * 4 + y
        return x * 4 + lax.rem(y + step + 4, 4)

    def shifted(index, axis, step):
        px, py = index // 4, index % 4
        if axis == 0:
            return lax.rem(px + step + 4, 4) * 4 + py
        return px * 4 + lax.rem(py + step + 4, 4)

    def part_of(index, half, part=None):
        first_row, n = (0, X_FIRST) if half == 0 else (X_FIRST, 16 - X_FIRST)
        if part is not None:
            n = n // 2
            first_row += part * n
        return new.at[pl.ds(index * 16 + first_row, n)]

    class Gather:
        def __init__(self, half):
            self.half, self.base = half, half * 20
            self.axes = (0, 1) if half == 0 else (1, 0)

        def copy(self, phase, item, role, index, part=None, step=None):
            n = self.base + phase * (1 + item) * 4 + role
            ref = part_of(index, self.half, part)
            if step is None:
                step = 1 if role % 2 == 0 else 3
            return remote(ref, ref, s_ag.at[n], r_ag.at[n], (ring(self.axes[phase], step), col))

        def send(self, *args, **kw):
            copy = self.copy(*args, **kw)
            copy.start()
            sends.append(copy)

        def start(self, phase, item, index):
            for role in range(2):
                self.send(phase, item, role, index)
            if phase == 0:
                self.send(phase, item, 2, index, step=2)

        def near(self, phase, item, index, role):
            came = shifted(index, self.axes[phase], 3 if role == 0 else 1)
            self.copy(phase, item, role, came).wait_recv()
            if phase == 1:
                self.send(phase, item, 2 + role, came, role)
            return came

        def far(self, phase, item, index):
            came = shifted(index, self.axes[phase], 2)
            if phase == 0:
                self.copy(phase, item, 2, came, step=2).wait_recv()
                return came
            for role in range(2):
                self.copy(phase, item, 2 + role, came, role).wait_recv()
            return came

    exchanged(send_ref, got, k, s_got, r_got)
    own.wait()
    for i in range(16):
        new[me * 16 + i] = got[table_ref[T_PICK, i]]
    flat = new.reshape(NT * DEV, NB)

    def convert(dx, dy):
        index = at(x + dx, y + dy)[0]
        rows = pl.ds(pl.multiple_of(index * 16, 16), 16)
        for c in range(DEV):
            hi, lo = split(flat[pl.ds(index * 16 * DEV + c, 16, stride=DEV), :])
            b_hi[rows, c * NB : (c + 1) * NB] = hi
            b_lo[rows, c * NB : (c + 1) * NB] = lo

    halves = [Gather(h) for h in range(2)]
    items = [[me], [me]]
    for g in halves:
        g.start(0, 0, me)
    for g in halves:
        g.start(1, 0, me)

    def top_part(index):
        return top.at[core, pl.ds(index * 16, 16)]

    def top_send(j):
        return remote(top_part(me), top_part(me), s_top.at[j], r_top.at[j], plane[j])

    def spread(kind, i):
        ref = (top if kind == 0 else side).at[core]
        return remote(ref, ref, s_far.at[kind, i], r_far.at[kind], others[i])

    def pass_on(kind):
        ref = (top if kind == 0 else side).at[core]
        n = PIECES + kind
        return remote(ref, ref, s_sib.at[n], r_sib.at[n], sibling)

    def from_sibling(kind):
        ref = (top if kind == 0 else side).at[1 - core]
        n = PIECES + kind
        return remote(ref, ref, s_sib.at[n], r_sib.at[n], sibling)

    @pl.when(is_root)
    def _():
        top[core, pl.ds(me * 16, 16), :] = new.reshape(NT * DEV, NB)[
            pl.ds(me * 16 * DEV, 16, stride=DEV), :
        ]
        for j in range(len(plane)):
            top_send(j).start()

    convert(0, 0)
    for role in range(2):
        for h, g in enumerate(halves):
            came = g.near(0, 0, me, role)
            g.start(1, 1 + role, came)
            items[h].append(came)
    for h, g in enumerate(halves):
        came = g.far(0, 0, me)
        g.start(1, 3, came)
        items[h].append(came)

    for half in range(2):

        @pl.when(me == half)
        def _():
            deal_own(half).wait()

        @pl.when(me != half)
        def _():
            ref = mid.at[pl.ds(half * 8, 8)]
            remote(ref, ref, s_out.at[0], r_out.at[half], plane[0]).wait_recv()

    for i in range(DEV * both):
        leave2[i] = mid[table_ref[T_MID, i]]
    exchange(leave2, old, both, s_mid, r_mid)
    own_old = pltpu.make_async_copy(
        leave2.at[pl.ds(me * both, both)], old.at[pl.ds(me * both, both)], s_loc.at[4]
    )
    own_old.start()


    @pl.when(is_root)
    def _():
        for j in range(len(plane)):
            index = origin[j][0]
            remote(
                top_part(index), top_part(index), s_top.at[j], r_top.at[j], plane[j]
            ).wait_recv()
        for i in range(3):
            spread(0, i).start()
        pass_on(0).start()

    def forward(i):
        for h, g in enumerate(halves):
            for role in range(2):
                g.near(1, i, items[h][i], role)


    forward(0)
    forward(1)

    @pl.when(z > 0)
    def _():
        spread(0, 0).wait_recv()
        pass_on(0).start()

    forward(2)
    forward(3)
    for i in range(PIECES):
        z_step(i)
    exchanged(leave2, old, both, s_mid, r_mid)
    own_old.wait()
    outs = [
        pltpu.make_async_copy(old, old_out.at[pl.ds(0, DEV * both)], s_loc.at[5]),
        pltpu.make_async_copy(side_g, side_out.at[pl.ds(0, DEV * both)], s_loc.at[6]),
    ]
    outs[0].start()

    @pl.when(is_root)
    def _():
        side[core] = old.reshape(DEV * both * DEV, NB)[pl.ds(0, DEV * both, stride=DEV), :]
        for i in range(3):
            spread(1, i).start()
        pass_on(1).start()

    for i in range(PIECES):
        z_finish(i)
    from_sibling(0).wait_recv()

    place = place_ref[T_PLACE : T_PLACE + 1, :]
    order_t = jnp.where(iota((NT, NT), 0) == place, 1.0, 0.0).astype(jnp.bfloat16)

    def pick(lo, val):
        return lax.dot_general(
            order_t[:, lo : lo + NB], val, (((0,), (0,)), ((), ())),
            preferred_element_type=jnp.float32,
        ).astype(jnp.bfloat16)

    inv = [split(inv_ref[s]) for s in range(2)]
    u0p = tuple(pick(0, v) for v in split(top[1]))
    l0b_full = dot3(tuple(pick(NB, v) for v in split(top[0])), inv[0])
    l0b = split(l0b_full)

    def factors(p0, p1):
        l0 = dot3(split(p0), inv[0])
        l1 = dot3(split(p1 - dot3(split(l0), u0p)), inv[1])
        return l0, l0 - dot3(split(l1), l0b), l1

    def placed(g0, l1):
        return [
            lax.dot_general(
                val, order_t, (((1,), (1,)), ((), ())), preferred_element_type=jnp.float32
            )
            for val in split(jnp.concatenate([g0, l1], axis=1))
        ]

    def keep_factors(part, l0, g0, l1):
        fac_ref[part, :] = jnp.where(col == 0, l0, l1)
        for ref, val in zip((g_hi, g_lo), placed(g0, l1)):
            ref[part, :] = val.astype(jnp.bfloat16)

    for i in range(4):
        part = pl.ds(i * 256, 256)
        keep_factors(part, *factors(panel[0, part, :], panel[1, part, :]))

    unit = jnp.where(iota((NB, NB), 0) == iota((NB, NB), 1), -1.0, 0.0)
    none = jnp.zeros((NB, NB), jnp.float32)

    @pl.when(me == 0)
    def _():
        keep_factors(pl.ds(0, NB), none, unit, none)

    @pl.when(me == 1)
    def _():
        keep_factors(pl.ds(0, NB), l0b_full, l0b_full, unit)

    @pl.when(z > 0)
    def _():
        spread(1, 0).wait_recv()
        pass_on(1).start()

    from_sibling(1).wait_recv()
    l0, g0, l1 = factors(side[0], side[1])
    for val, lanes in zip(placed(g0, l1), (slice(0, NT), slice(NT, 2 * NT))):
        side_g[:, lanes] = val
    side_g[:, 2 * NT :] = jnp.where(col == 0, l0, l1)
    outs[1].start()
    for dx, dy in offsets:
        if dx != 2 and dy != 2:
            convert(dx, dy)
    for i in range(4):
        for h, g in enumerate(halves):
            g.far(1, i, items[h][i])
    for dx, dy in offsets:
        if dx == 2 or dy == 2:
            convert(dx, dy)

    for kind in range(2):
        pass_on(kind).wait_send()

    @pl.when(is_root)
    def _():
        for kind in range(2):
            for i in range(3):
                spread(kind, i).wait_send()
        for i in range(PIECES):
            for j in range(3):
                z_out(i, j).wait_send()
        for j in range(len(plane)):
            top_send(j).wait_send()

    for half in range(2):

        @pl.when(me == half)
        def _():
            for copy in deal_out(half):
                copy.wait_send()

    for copy in sends:
        copy.wait_send()
    for copy in outs:
        copy.wait()


def move(k, table, inverses, send, work):
    both = OLD[k]
    dma = pltpu.SemaphoreType.DMA
    f32, b16 = jnp.float32, jnp.bfloat16
    outs = (
        ((NT, DEV * NB), b16), ((NT, DEV * NB), b16),
        ((ROWS, NT), b16), ((ROWS, NT), b16), ((ROWS, NB), f32),
        ((N_OLD[MANY], DEV, NB), f32), ((N_OLD[MANY], 2 * NT + NB), f32),
    )
    scratch = (
        (DEV * k, DEV, NB), (16, DEV, NB), (NB, DEV, NB), (DEV * both, DEV, NB), (NB, DEV, NB),
        (ROWS, 8, NB), (NT, DEV, NB), (2, ROWS, NB), (2, NT, NB), (2, DEV * both, NB), (DEV * both, DEV, NB),
        (DEV * both, 2 * NT + NB),
    )
    any_ = pl.BlockSpec(memory_space=pl.ANY)
    vmem = pl.BlockSpec(memory_space=pltpu.VMEM)
    return pl.pallas_call(
        functools.partial(move_kernel, k),
        out_shape=tuple(jax.ShapeDtypeStruct(*s) for s in outs),
        in_specs=[pl.BlockSpec(memory_space=pltpu.SMEM), vmem, vmem, any_, any_],
        out_specs=(vmem,) * 5 + (pl.BlockSpec(memory_space=pltpu.HBM),) * 2,
        scratch_shapes=[pltpu.VMEM(s, jnp.float32) for s in scratch]
        + [
            dma((15,)), dma((15,)), dma((15,)), dma((2,)), dma((15,)), dma((15,)),
            dma((40,)), dma((40,)), dma((PIECES, 3)), dma((PIECES,)),
            dma((PIECES + 2,)), dma((PIECES + 2,)), dma((15,)), dma((15,)),
            dma((2, 3)), dma((2,)), dma((7,)),
        ],
        compiler_params=pltpu.CompilerParams(
            collective_id=k, has_side_effects=True, vmem_limit_bytes=(18 if k == FEW else 24) * MIB
        ),
        name=f"move_{k}",
    )(table, table, inverses, send, work)


CHUNKS = 4
CROWS = ROWS // CHUNKS
PITCH = 24


def update_kernel(
    table_ref, a_ref, b_hi, b_lo, hi_ref, lo_ref, fac_ref, old_ref, side_ref,
    out_ref,
    a, g_hi, g_lo, fac, old, side, sems, old_sems,
):
    me = lax.axis_index("prow")
    col = lax.axis_index("pcol")
    few = table_ref[T_OVER, 0] == 0
    parts = [pl.ds(i * CROWS, CROWS) for i in range(CHUNKS)]

    def old_loads(n):
        part = pl.ds(0, n)
        return [
            pltpu.make_async_copy(old_ref.at[part], old.at[part], old_sems.at[0]),
            pltpu.make_async_copy(side_ref.at[part], side.at[part], old_sems.at[1]),
        ]

    def each_old(do):
        for cond, k in ((few, FEW), (jnp.logical_not(few), MANY)):

            @pl.when(cond)
            def _():
                for copy in old_loads(N_OLD[k]):
                    do(copy)

    each_old(lambda copy: copy.start())
    loads = [
        pltpu.make_async_copy(a_ref.at[part], a.at[part, pl.ds(0, DEV)], sems.at[i])
        for i, part in enumerate(parts)
    ]
    for copy in loads[:2]:
        copy.start()

    def each_fix(fix):
        @pl.loop(0, table_ref[T_COUNT, 0])
        def _(i):
            entry = table_ref[T_FIX, i]
            src = entry & (NT - 1)
            packed = (src >> 4) * OLD[FEW] + (src & (DEV - 1))
            fix(entry >> 8, jnp.where(few, packed, src))

    aflat = a.reshape(ROWS * PITCH, NB)
    g_hi[...] = hi_ref[...].astype(jnp.float32)
    g_lo[...] = lo_ref[...].astype(jnp.float32)
    fac[...] = fac_ref[...]

    def fix_factors(dst, src):
        row = side[pl.ds(src, 1), :]
        g_hi[pl.ds(dst, 1), :] = row[:, :NT]
        g_lo[pl.ds(dst, 1), :] = row[:, NT : 2 * NT]
        fac[pl.ds(dst, 1), :] = row[:, 2 * NT :]

    each_old(lambda copy: copy.wait())
    each_fix(fix_factors)
    stores = []
    for i, part in enumerate(parts):
        hi, lo = g_hi[part, :].astype(jnp.bfloat16), g_lo[part, :].astype(jnp.bfloat16)
        left = jnp.concatenate([hi, hi, lo], axis=1)
        loads[i].wait()
        if i + 2 < CHUNKS:
            loads[i + 2].start()

        def fix_row(dst, src):
            @pl.when(dst // CROWS == i)
            def _():
                a[dst, 0:DEV, :] = old[src]

        each_fix(fix_row)
        if i == 0:
            @pl.when(me < 2)
            def _():
                a[0:NB, 0:DEV, :] = jnp.zeros((NB, DEV, NB), jnp.float32)

        for c in range(0, DEV, 2):
            wide = slice(c * NB, (c + 2) * NB)
            right = jnp.concatenate([b_hi[:, wide], b_lo[:, wide], b_hi[:, wide]], axis=0)
            upd = dot(left, right)
            for h in range(2):
                where = pl.ds(i * CROWS * PITCH + c + h, CROWS, stride=PITCH)
                val = aflat[where, :] - upd[:, h * NB : (h + 1) * NB]
                if c + h == 0:
                    own = fac[part, :]
                    if i == 0:
                        keep = jnp.where(col == 0, me == 0, me < 2)
                        own = jnp.where((iota((CROWS, NB), 0) < NB) & keep, val, own)
                    val = jnp.where(col < 2, own, val)
                aflat[where, :] = val
        store = pltpu.make_async_copy(
            a.at[part, pl.ds(0, DEV)], out_ref.at[part], sems.at[CHUNKS + i]
        )
        store.start()
        stores.append(store)
    for store in stores:
        store.wait()


def update(table, work, *moved):
    any_ = pl.BlockSpec(memory_space=pl.ANY)
    vmem = pl.BlockSpec(memory_space=pltpu.VMEM)
    return pl.pallas_call(
        update_kernel,
        out_shape=jax.ShapeDtypeStruct((ROWS, DEV, NB), jnp.float32),
        in_specs=[pl.BlockSpec(memory_space=pltpu.SMEM), any_] + [vmem] * 5 + [pl.BlockSpec(memory_space=pltpu.HBM)] * 2,
        out_specs=any_,
        scratch_shapes=[
            pltpu.VMEM((ROWS, PITCH, NB), jnp.float32),
            pltpu.VMEM((ROWS, NT), jnp.float32),
            pltpu.VMEM((ROWS, NT), jnp.float32),
            pltpu.VMEM((ROWS, NB), jnp.float32),
            pltpu.VMEM((N_OLD[MANY], DEV, NB), jnp.float32),
            pltpu.VMEM((N_OLD[MANY], 2 * NT + NB), jnp.float32),
            pltpu.SemaphoreType.DMA((2 * CHUNKS,)),
            pltpu.SemaphoreType.DMA((2,)),
        ],
        compiler_params=pltpu.CompilerParams(vmem_limit_bytes=24 * MIB),
        name="update",
    )(table, work, *moved)


def on_device(matrix, pivots, block_inverses):
    work = matrix.reshape(ROWS, DEV, NB)
    table, send, over = plan(FEW, pivots, work)

    def few():
        return move(FEW, table, block_inverses, send, work)

    def many():
        other, rows, _ = plan(MANY, pivots, work)
        return move(MANY, other, block_inverses, rows, work)

    moved = lax.cond(over.reshape(()) == 0, few, many)
    out = update(table, work, *moved)
    return out.reshape(matrix.shape)


def solution(mesh):
    in_specs = (P(None, "prow", None, None, "pcol", None), P(), P())
    out_specs = P(None, "prow", None, None, "pcol", None)
    return jax.shard_map(
        on_device, mesh=mesh, in_specs=in_specs, out_specs=out_specs, check_vma=False
    )
```
